32 devices in a mesh: rep: 4 (over y, x), fsdp: 8 (over z, core).
Axes of the slice: x: 2, y: 2, z: 4, core: 2. Of those that a mesh axis runs over, the one named last changes fastest.
Arguments:
- tokens: bfloat16 [10240, 2048], P(('rep', 'fsdp')), may hold values from -6 to 6
- lengths: int32 [4, 2], P('rep'), may hold values from 1024 to 1536, as said below
- dealing: int32 [10240], P('rep'), may hold values from 0 to 2559, as said below
- routes: int32 [10240, 4], P('rep'), may hold values from 0 to 7, all different within a row; in each aligned block of 320 rows (0 to 319, 320 to 639, ...) at most 192 rows name the same one
- cotangent: bfloat16 [10240, 2048], P(('rep', 'fsdp')), may hold values from -6 to 6
- first_gain: bfloat16 [2048], P('fsdp'), may hold values from 0.5 to 1.5
- projection: bfloat16 [2048, 6144], P('fsdp'), may hold values from -0.125 to 0.125
- projection_bias: bfloat16 [6144], P('fsdp'), may hold values from -0.59765625 to 0.59765625
- output_weight: bfloat16 [2048, 2048], P('fsdp'), may hold values from -1.25 to 1.25
- second_gain: bfloat16 [2048], P('fsdp'), may hold values from 0.5 to 1.5
- router_weight: bfloat16 [2048, 8], P('fsdp'), may hold values from -0.0625 to 0.0625
- shared_gate: bfloat16 [2048], P('fsdp'), may hold values from -0.125 to 0.125
- shared_in: bfloat16 [2, 2048, 5632], P(None, None, 'fsdp'), may hold values from -0.125 to 0.125
- shared_out: bfloat16 [5632, 2048], P('fsdp'), may hold values from -0.15625 to 0.15625
- expert_in: bfloat16 [8, 2, 2048, 1408], P(None, None, None, 'fsdp'), may hold values from -0.125 to 0.125
- expert_out: bfloat16 [8, 1408, 2048], P(None, 'fsdp'), may hold values from -0.4375 to 0.4375
Outputs:
- mixed: bfloat16 [10240, 2048], P(('rep', 'fsdp'))
- tokens_grad: float32 [10240, 2048], P(('rep', 'fsdp'))
- first_gain_grad: float32 [2048], P('fsdp')
- projection_grad: float32 [2048, 6144], P('fsdp')
- projection_bias_grad: float32 [6144], P('fsdp')
- output_weight_grad: float32 [2048, 2048], P('fsdp')
- second_gain_grad: float32 [2048], P('fsdp')
- router_weight_grad: float32 [2048, 8], P('fsdp')
- shared_gate_grad: float32 [2048], P('fsdp')
- shared_in_grad: float32 [2, 2048, 5632], P(None, None, 'fsdp')
- shared_out_grad: float32 [5632, 2048], P('fsdp')
- expert_in_grad: float32 [8, 2, 2048, 1408], P(None, None, None, 'fsdp')
- expert_out_grad: float32 [8, 1408, 2048], P(None, 'fsdp')
The draws below stay inside these ranges and needn't reach their ends.
Inputs may be any that keep to these rules, and one draw needn't show every extreme that they name: A group's two lengths add up to 2560; the first group's first sequence has exactly 1024 tokens. `dealing`: within a group's 2560 rows every value stands once; the k-th of a device's 320 rows holds a value from 8 * k to 8 * k + 7. `routes`: A row names 4 different experts; in each aligned block of 320 rows (one device's rows) no expert is named by more than 192 rows, and in some blocks one is named by exactly 192.
All inputs are finite; a program needn't handle non-finite values.
Results may differ from the reference program's by a relative error of at most 0.018.
Values may be sent and summed in bfloat16 or wider, within the bound.
A program may use at most 576 MiB of HBM per device.

```python
import math
from functools import partial
import jax
import jax.numpy as jnp
import numpy as np
from jax import lax

D = 2048
HEADS = 16
HEAD_DIM = 128
FS = 5632
FE = 1408
TOP = 4
EXPERTS = 8
MIN_LEN = 1024
GROUP_TOK = 2560
TOK_DEV = 320
GROUPS = 4
TOKENS = 10240
CAP = 192


def draw_lengths(key, part):
    key = jax.random.fold_in(key, 11)
    first = jax.random.randint(key, (GROUPS,), MIN_LEN, GROUP_TOK - MIN_LEN + 1, dtype=jnp.int32)
    first = first.at[0].set(MIN_LEN)
    return jnp.stack([first, GROUP_TOK - first], axis=1).astype(jnp.int32)


def draw_dealing(key, part):
    key = jax.random.fold_in(key, 12)
    spread = GROUP_TOK // TOK_DEV
    scores = jax.random.randint(key, (GROUPS, TOK_DEV, spread), 0, 1 << 20, dtype=jnp.int32) * spread + jnp.arange(spread, dtype=jnp.int32)
    order = jnp.argsort(scores, axis=-1).astype(jnp.int32)
    placed = jnp.transpose(order, (0, 2, 1)) + spread * jnp.arange(TOK_DEV, dtype=jnp.int32)[None, None, :]
    return placed.reshape(GROUPS * GROUP_TOK).astype(jnp.int32)


def steps_of(stream_key, extent, pieces, smallest, top_value):
    factor_of = 1.0
    for dim, parts in pieces:
        draws = jax.random.uniform(jax.random.fold_in(jax.random.fold_in(stream_key, 6), dim), (parts,), jnp.float32, smallest / len(pieces), top_value / len(pieces))
        factor_of = factor_of * jnp.repeat(jnp.exp(draws), extent[dim] // parts).reshape((-1,) + (1,) * (len(extent) - 1 - dim))
    return factor_of


def deal_out(own_key, own, number, rows, count, top, bound, slope):
    order = jax.random.permutation(own_key, count)
    heavy_load, common = shares(count, rows * top, bound, slope, True), shares(count, rows * top, bound, slope, False)
    places = jnp.arange(count)

    def named(tallies, rotation):
        used = int((tallies > 0).sum())
        fixed = max(1, used // 4)
        moved = fixed + (places - fixed + rotation * (used - fixed)) % max(1, count - fixed)
        return jnp.zeros((count,), jnp.int32).at[order[jnp.where(places < fixed, places, moved)]].set(jnp.asarray(tallies, jnp.int32))

    tallies = jnp.where(number % 4 == 0, named(heavy_load, number // 4), named(common, number - number // 4 - 1))
    mixed = jax.random.permutation(jax.random.fold_in(own, 3), count)
    donor, sink = mixed[0:count // 2 * 2:2], mixed[1:count // 2 * 2:2]
    room = jnp.minimum(tallies[donor] - 1, bound - tallies[sink]) // 2
    room = jnp.where((donor == order[0]) | (sink == order[0]) | (tallies[sink] == 0), 0, jnp.maximum(room, 0))
    moved = jax.random.randint(jax.random.fold_in(own, 4), (count // 2,), 0, 1 << 20) % (room + 1)
    tallies = tallies.at[donor].add(-moved).at[sink].add(moved)
    labels = jnp.searchsorted(jnp.cumsum(tallies), jnp.arange(rows * top), side="right").astype(jnp.int32)
    table = labels.reshape(top, rows).T
    table = table[jax.random.permutation(jax.random.fold_in(own, 1), rows)]
    rotation = jax.random.randint(jax.random.fold_in(own, 2), (rows, 1), 0, top)
    return jnp.take_along_axis(table, (jnp.arange(top)[None, :] + rotation) % top, axis=1)


def shares(count, total, reach, skew, full):
    portions = [(1 << 20) // math.isqrt(rank ** skew) + 1 for rank in range(1, count + 1)]
    largest = reach if full else min(reach, max(-(-total // count), total * portions[0] // sum(portions)))
    least = 1 if total - largest >= count - 1 else 0
    holding, surplus = [largest] + [least] * (count - 1), total - largest - least * (count - 1)
    while surplus > 0:
        movable = [i for i in range(1, count) if holding[i] < largest] or [i for i in range(1, count) if holding[i] < reach]
        whole, left = sum([portions[i] for i in movable]), surplus
        for i in movable:
            extra = min(reach - holding[i], max(1, left * portions[i] // whole), surplus)
            holding[i] = holding[i] + extra
            surplus = surplus - extra
    return np.array(holding)


def bell_draw(stream_key, dims, scale, bound, cuts=(), kind=jnp.bfloat16):
    entries = jax.random.normal(stream_key, dims, jnp.float32) * scale
    if len(cuts) > 0:
        entries = steps_of(stream_key, dims, cuts, -0.22, 0.18) * entries
    return jnp.clip(entries, min=-bound, max=bound).astype(kind)


def setup_inputs(seed: int = 0) -> dict:
    splits = jax.random.split(jax.random.key(seed), 17)
    tokens = bell_draw(splits[0], (TOKENS, D), 1.0, 6.0, ((0, 32),))
    lengths = draw_lengths(jax.random.fold_in(splits[16], 71), 0)
    dealing = draw_dealing(jax.random.fold_in(splits[16], 71), 0)
    routes_keys = jax.random.split(jax.random.fold_in(splits[3], 1), TOKENS // TOK_DEV)
    routes_turns = jax.random.permutation(jax.random.fold_in(splits[3], 3), TOKENS // TOK_DEV)
    routes = jax.vmap(lambda own, number: deal_out(jax.random.fold_in(splits[3], 2), own, number, TOK_DEV, EXPERTS, TOP, CAP, 1))(routes_keys, routes_turns).reshape((TOKENS, TOP))
    cotangent = bell_draw(splits[4], (TOKENS, D), 1.0, 6.0, ((0, 32),))
    first_gain = jnp.clip(1.0 + 0.1 * jax.random.normal(splits[5], (D,), jnp.float32), 0.5, 1.5).astype(jnp.bfloat16)
    projection = bell_draw(splits[6], (D, 3 * D), D ** -0.5, 0.125, ((0, 8),))
    projection_bias = bell_draw(splits[7], (3 * D,), 0.1, 0.59765625, ((0, 8),))
    output_weight = bell_draw(splits[8], (D, D), (max(D * 32 // GROUP_TOK, 1)) ** -0.5, 1.25, ((0, 8),))
    second_gain = jnp.clip(1.0 + 0.1 * jax.random.normal(splits[9], (D,), jnp.float32), 0.5, 1.5).astype(jnp.bfloat16)
    router_weight = bell_draw(splits[10], (D, EXPERTS), (4 * D) ** -0.5, 0.0625, ((0, 8),))
    shared_gate = bell_draw(splits[11], (D,), D ** -0.5, 0.125, ((0, 8),))
    shared_in = bell_draw(splits[12], (2, D, FS), D ** -0.5, 0.125, ((2, 8),))
    shared_out = bell_draw(splits[13], (FS, D), (FS // 4) ** -0.5, 0.15625, ((0, 8),))
    expert_in = bell_draw(splits[14], (EXPERTS, 2, D, FE), D ** -0.5, 0.125, ((3, 8),))
    expert_out = bell_draw(splits[15], (EXPERTS, FE, D), (FE // 8) ** -0.5, 0.4375, ((1, 8),))
    return {"tokens": tokens, "lengths": lengths, "dealing": dealing, "routes": routes, "cotangent": cotangent, "first_gain": first_gain, "projection": projection, "projection_bias": projection_bias, "output_weight": output_weight, "second_gain": second_gain, "router_weight": router_weight, "shared_gate": shared_gate, "shared_in": shared_in, "shared_out": shared_out, "expert_in": expert_in, "expert_out": expert_out}


EPS = 1e-06
THETA = 1000000.0
NEG = -1e+30
HIGHEST_PRECISION = lax.Precision.HIGHEST

@jax.custom_vjp
def low(v):
    return lax.optimization_barrier(v.astype(jnp.bfloat16)).astype(jnp.float32)

@jax.custom_vjp
def low_back(v):
    return v

def low_keep(v):
    return (low(v), None)

def low_pass(kept, grad):
    return (grad,)

def back_keep(v):
    return (v, None)

def back_low(kept, grad):
    return (low(grad),)
low.defvjp(low_keep, low_pass)
low_back.defvjp(back_keep, back_low)

def matmul(left, right):
    return jnp.dot(left, right, precision=HIGHEST_PRECISION)

def rms(values, gain):
    return values * lax.rsqrt(lax.optimization_barrier(jnp.mean(values * values, axis=-1, keepdims=True)) + EPS) * gain

def rope_tables(position, size):
    half = size // 2
    freq = THETA ** (-(jnp.arange(half, dtype=jnp.float32) * (2.0 / size)))
    angle = position.astype(jnp.float32)[:, None] * freq[None, :]
    return (jnp.cos(angle), jnp.sin(angle))

def rotate(values, cosine, sine):
    half = values.shape[-1] // 2
    first = values[..., :half]
    second = values[..., half:]
    cos_part = cosine[:, None, :]
    sin_part = sine[:, None, :]
    return jnp.concatenate([first * cos_part - second * sin_part, second * cos_part + first * sin_part], axis=-1)

def gated(gate_values, up_values):
    return jax.nn.silu(gate_values) * up_values

def expert_slots(routes, experts, capacity):
    pairs = routes.reshape(-1).astype(jnp.int32)
    total = pairs.shape[0]
    member = (pairs[:, None] == jnp.arange(experts, dtype=jnp.int32)[None, :]).astype(jnp.int32)
    before = (jnp.cumsum(member, axis=0) - member).astype(jnp.int32)
    within = lax.optimization_barrier(jnp.sum(before * member, axis=1)).astype(jnp.int32)
    slot = (pairs * capacity + within).astype(jnp.int32)
    source = jnp.full((experts * capacity,), total, jnp.int32).at[slot].set(jnp.arange(total, dtype=jnp.int32))
    return (slot, source)

def group_attention(inputs):
    query, keys, values, stream, second = inputs
    scores = low_back(jnp.einsum('qhd,khd->hqk', query, keys, precision=HIGHEST_PRECISION) * HEAD_DIM ** (-0.5))
    visible = (second[:, None] == second[None, :]) & (stream[None, :] <= stream[:, None])
    scores = jnp.where(visible[None], scores, NEG)
    shifted = jnp.exp(scores - lax.optimization_barrier(jnp.max(scores, axis=-1, keepdims=True)))
    probs = shifted / lax.optimization_barrier(jnp.sum(shifted, axis=-1, keepdims=True))
    return jnp.einsum('hqk,khd->qhd', low(probs), values, precision=HIGHEST_PRECISION)

def expert_apply(inputs):
    rows_in, weight_in, weight_down = inputs
    mixture = low_back(jnp.einsum('rd,cdf->rcf', rows_in, weight_in, precision=HIGHEST_PRECISION))
    activation = low(gated(mixture[:, 0], mixture[:, 1]))
    return low_back(matmul(activation, weight_down))

def take_rows(block, index):
    return jnp.take(block, index, axis=0)

def forward(params, inputs, lengths, dealing, routes):
    first_gain, projection, projection_bias, output_weight, second_gain, router_weight, shared_gate, shared_in, shared_out, expert_in, expert_out = params
    group_of = jnp.arange(TOKENS, dtype=jnp.int32) // GROUP_TOK
    first_length = lengths[group_of, 0]
    second = (dealing >= first_length).astype(jnp.int32)
    position = (dealing - second * first_length).astype(jnp.int32)
    cosine, sine = rope_tables(position, HEAD_DIM)
    hidden_one = low(rms(inputs, first_gain))
    projected = low_back(matmul(hidden_one, projection) + projection_bias)
    query = projected[:, :D].reshape(TOKENS, HEADS, HEAD_DIM)
    keyed = projected[:, D:2 * D].reshape(TOKENS, HEADS, HEAD_DIM)
    valued = projected[:, 2 * D:].reshape(TOKENS, HEADS, HEAD_DIM)
    query_low = low(rotate(query, cosine, sine))
    key_low = low(rotate(keyed, cosine, sine))
    value_low = low(valued)
    grouped = (GROUPS, GROUP_TOK, HEADS, HEAD_DIM)
    attended = lax.map(jax.checkpoint(group_attention), (query_low.reshape(grouped), key_low.reshape(grouped), value_low.reshape(grouped), dealing.reshape(GROUPS, GROUP_TOK), second.reshape(GROUPS, GROUP_TOK)))
    attended = low(low_back(attended.reshape(TOKENS, D)))
    residual = inputs + low_back(matmul(attended, output_weight))
    hidden_two = low(rms(residual, second_gain))
    logits = matmul(hidden_two, router_weight)
    shifted = jnp.exp(logits - lax.optimization_barrier(jnp.max(logits, axis=-1, keepdims=True)))
    router_probs = shifted / lax.optimization_barrier(jnp.sum(shifted, axis=-1, keepdims=True))
    gates = jnp.take_along_axis(router_probs, routes, axis=1)
    sigma = jax.nn.sigmoid(matmul(hidden_two, shared_gate))
    shared_mix = low_back(jnp.einsum('nd,cdf->ncf', hidden_two, shared_in, precision=HIGHEST_PRECISION))
    shared_act = low(gated(shared_mix[:, 0], shared_mix[:, 1]))
    shared_y = low_back(matmul(shared_act, shared_out))
    blocks = TOKENS // TOK_DEV
    slot, source = jax.vmap(partial(expert_slots, experts=EXPERTS, capacity=CAP))(routes.reshape(blocks, TOK_DEV, TOP))
    padded = jnp.concatenate([hidden_two.reshape(blocks, TOK_DEV, D), jnp.zeros((blocks, 1, D), jnp.float32)], axis=1)
    expert_rows = jax.vmap(take_rows)(padded, source // TOP)
    expert_rows = expert_rows.reshape(blocks, EXPERTS, CAP, D).transpose(1, 0, 2, 3).reshape(EXPERTS, blocks * CAP, D)
    expert_y = lax.map(jax.checkpoint(expert_apply), (expert_rows, expert_in, expert_out))
    expert_y = expert_y.reshape(EXPERTS, blocks, CAP, D).transpose(1, 0, 2, 3).reshape(blocks, EXPERTS * CAP, D)
    picked = jax.vmap(take_rows)(expert_y, slot).reshape(TOKENS, TOP, D)
    routed = lax.optimization_barrier(jnp.sum(gates[:, :, None] * picked, axis=1))
    return residual + sigma[:, None] * shared_y + routed

def reference(tokens, lengths, dealing, routes, cotangent, first_gain, projection, projection_bias, output_weight, second_gain, router_weight, shared_gate, shared_in, shared_out, expert_in, expert_out):
    params = tuple((weight.astype(jnp.float32) for weight in (first_gain, projection, projection_bias, output_weight, second_gain, router_weight, shared_gate, shared_in, shared_out, expert_in, expert_out)))
    inputs = tokens.astype(jnp.float32)

    def run(weights, values):
        return forward(weights, values, lengths, dealing, routes)
    output, pullback = jax.vjp(run, params, inputs)
    weight_grads, tokens_grad = pullback(cotangent.astype(jnp.float32))
    return (output.astype(jnp.bfloat16), tokens_grad, weight_grads[0], weight_grads[1], weight_grads[2], weight_grads[3], weight_grads[4], weight_grads[5], weight_grads[6], weight_grads[7], weight_grads[8], weight_grads[9], weight_grads[10])
```

```python
import functools

import jax
import jax.numpy as jnp
from jax import lax
from jax.experimental import pallas as pl
from jax.experimental.pallas import tpu as pltpu
from jax.sharding import PartitionSpec as P

HEAD_DIM = 128
EPS = 1e-06
THETA = 1000000.0
NEG = -1e30
LOW = jnp.bfloat16
WIDE = jnp.float32


def dot(left, right, dims, kind=WIDE):
    return lax.dot_general(left, right, ((dims[0], dims[1]), ((), ())), preferred_element_type=kind)


def mm(left, right, kind=WIDE):
    return dot(left, right, ((1,), (0,)), kind)


def mm_nt(left, right, kind=WIDE):
    return dot(left, right, ((1,), (1,)), kind)


def mm_tn(left, right, kind=WIDE):
    return dot(left, right, ((0,), (0,)), kind)


def scale_of(values):
    return lax.rsqrt(jnp.mean(values * values, axis=-1, keepdims=True) + EPS)


def rope_tables(position):
    half = HEAD_DIM // 2
    freq = THETA ** (-(jnp.arange(half, dtype=WIDE) * (2.0 / HEAD_DIM)))
    angle = position.astype(WIDE)[:, None] * freq[None, :]
    return (jnp.cos(angle), jnp.sin(angle))


def pair_block(ref, index, size):
    block = ref[:, pl.ds(pl.multiple_of(index * size, size), size), :]
    return block.reshape(block.shape[0] * size, block.shape[2])


def put_block(ref, index, size, block):
    ref[:, pl.ds(pl.multiple_of(index * size, size), size), :] = block.reshape(
        ref.shape[0], size, block.shape[1]
    )


def first_block(first_length, index, width):
    return jnp.where(index * width >= first_length, first_length // width, 0)


def span_mask(at_col, at_row, first_length):
    lowest = jnp.where(at_col >= first_length, first_length, 0)
    return (at_row <= at_col) & (at_row >= lowest)


def attend_kernel(
    size,
    lengths,
    query_in,
    key_in,
    value_in,
    cosine,
    sine,
    at_col,
    at_row,
    query,
    keyed,
    value,
    out,
    log_total,
):
    devices, rows, _ = query_in.shape
    width = size * devices
    first_length = lengths[0]
    factor = HEAD_DIM ** (-0.5)

    def prepare(index, carry):
        wave, ripple = pair_block(cosine, index, size), pair_block(sine, index, size)
        for source, target in ((query_in, query), (key_in, keyed)):
            block = pair_block(source, index, size)
            block = block * wave + pltpu.roll(block, HEAD_DIM // 2, 1) * ripple
            put_block(target, index, size, block.astype(LOW))
        put_block(value, index, size, pair_block(value_in, index, size).astype(LOW))
        return carry

    lax.fori_loop(0, rows // size, prepare, 0)

    def for_queries(index, carry):
        block = pair_block(query, index, size)
        places = pair_block(at_col, index, size)[:, :1]

        def for_keys(other, state):
            peak, total, summed = state
            raw = mm_nt(block, pair_block(keyed, other, size)) * factor
            raw = jnp.where(span_mask(places, at_row[other], first_length), raw, NEG)
            higher = jnp.maximum(peak, jnp.max(raw, axis=1, keepdims=True))
            lifted = jnp.exp(raw - higher)
            fade = jnp.exp(peak - higher)
            total = total * fade + jnp.sum(lifted, axis=1, keepdims=True)
            summed = summed * fade + mm(lifted.astype(LOW), pair_block(value, other, size))
            return higher, total, summed

        start = (
            jnp.full((width, 1), 2 * NEG, WIDE),
            jnp.zeros((width, 1), WIDE),
            jnp.zeros((width, HEAD_DIM), WIDE),
        )
        lowest = first_block(first_length, index, width)
        peak, total, summed = lax.fori_loop(lowest, index + 1, for_keys, start)
        put_block(out, index, size, (summed / total).astype(LOW))
        put_block(
            log_total, index, size, jnp.broadcast_to(peak + jnp.log(total), (width, HEAD_DIM))
        )
        return carry

    lax.fori_loop(0, rows // size, for_queries, 0)


def attend_back_kernel(
    size,
    lengths,
    query,
    keyed,
    value,
    attended,
    attended_back,
    log_total,
    cosine,
    sine,
    scale_row,
    at_col,
    at_row,
    query_back,
    key_back,
    value_back,
    query_scaled,
    key_scaled,
    value_scaled,
    query_sum,
    key_sum,
    value_sum,
):
    devices, rows, _ = query.shape
    width = size * devices
    first_length = lengths[0]
    factor = HEAD_DIM ** (-0.5)
    key_sum[...] = jnp.zeros_like(key_sum)
    value_sum[...] = jnp.zeros_like(value_sum)

    def for_queries(index, carry):
        block = pair_block(query, index, size)
        places = pair_block(at_col, index, size)[:, :1]
        logs = pair_block(log_total, index, size)[:, :1]
        pushed = pair_block(attended_back, index, size)
        row_dot = jnp.sum(
            pushed.astype(WIDE) * pair_block(attended, index, size).astype(WIDE),
            axis=1,
            keepdims=True,
        )

        def for_keys(other, summed):
            key_block = pair_block(keyed, other, size)
            raw = mm_nt(block, key_block) * factor
            raw = jnp.where(span_mask(places, at_row[other], first_length), raw, NEG)
            probs = jnp.exp(raw - logs)
            prob_back = mm_nt(pushed, pair_block(value, other, size))
            score_back = (probs * (prob_back - row_dot)).astype(LOW)
            here = pl.ds(pl.multiple_of(other * width, width), width)
            value_sum[here, :] += mm_tn(probs.astype(LOW), pushed)
            key_sum[here, :] += mm_tn(score_back, block)
            return summed + mm(score_back, key_block)

        lowest = first_block(first_length, index, width)
        query_sum[pl.ds(pl.multiple_of(index * width, width), width), :] = lax.fori_loop(
            lowest, index + 1, for_keys, jnp.zeros((width, HEAD_DIM), WIDE)
        )
        return carry

    lax.fori_loop(0, rows // size, for_queries, 0)

    def finish(index, carry):
        wave, ripple = pair_block(cosine, index, size), pair_block(sine, index, size)
        scale = pair_block(scale_row, index, size)[:, :1]
        here = pl.ds(pl.multiple_of(index * width, width), width)
        for source, target, scaled in (
            (query_sum, query_back, query_scaled),
            (key_sum, key_back, key_scaled),
        ):
            block = source[here, :] * factor
            block = block * wave - pltpu.roll(block, HEAD_DIM // 2, 1) * ripple
            block = block.astype(LOW)
            put_block(target, index, size, block)
            put_block(scaled, index, size, (block.astype(WIDE) * scale).astype(LOW))
        block = value_sum[here, :].astype(LOW)
        put_block(value_back, index, size, block)
        put_block(value_scaled, index, size, (block.astype(WIDE) * scale).astype(LOW))
        return carry

    lax.fori_loop(0, rows // size, finish, 0)


def work(micros):
    return pl.CostEstimate(
        flops=int(micros * 1e9), bytes_accessed=int(micros * 3e6), transcendentals=0
    )


def head_spec(devices, rows, first):
    return pl.BlockSpec((devices, rows, HEAD_DIM), lambda head: (0, 0, first + head))


def attend(lengths, projected, cosine, sine, at_col, at_row, held, size):
    devices, rows, _ = projected.shape
    whole = pl.BlockSpec((devices, rows, HEAD_DIM), lambda head: (0, 0, 0))
    low = jax.ShapeDtypeStruct((devices, rows, held * HEAD_DIM), LOW)
    return pl.pallas_call(
        functools.partial(attend_kernel, size),
        grid=(held,),
        in_specs=[
            pl.BlockSpec(memory_space=pltpu.SMEM),
            head_spec(devices, rows, 0),
            head_spec(devices, rows, held),
            head_spec(devices, rows, 2 * held),
            whole,
            whole,
            whole,
            pl.BlockSpec(at_row.shape, lambda head: (0, 0, 0)),
        ],
        out_specs=[head_spec(devices, rows, 0)] * 5,
        out_shape=[low] * 4 + [jax.ShapeDtypeStruct(low.shape, WIDE)],
        cost_estimate=work(30),
        compiler_params=pltpu.CompilerParams(vmem_limit_bytes=48 * 2**20),
    )(lengths, projected, projected, projected, cosine, sine, at_col, at_row)


def attend_back(
    lengths, query, keyed, value, attended, pushed, log_total, cosine, sine, scale_row,
    at_col, at_row, held, size,
):
    devices, rows, _ = query.shape
    whole = pl.BlockSpec((devices, rows, HEAD_DIM), lambda head: (0, 0, 0))
    own = head_spec(devices, rows, 0)
    low = jax.ShapeDtypeStruct((devices, rows, held * HEAD_DIM), LOW)
    return pl.pallas_call(
        functools.partial(attend_back_kernel, size),
        grid=(held,),
        in_specs=[
            pl.BlockSpec(memory_space=pltpu.SMEM),
            own,
            own,
            own,
            own,
            own,
            own,
            whole,
            whole,
            whole,
            whole,
            pl.BlockSpec(at_row.shape, lambda head: (0, 0, 0)),
        ],
        out_specs=[own] * 6,
        out_shape=[low] * 6,
        scratch_shapes=[pltpu.VMEM((devices * rows, HEAD_DIM), WIDE)] * 3,
        compiler_params=pltpu.CompilerParams(vmem_limit_bytes=48 * 2**20),
    )(
        lengths, query, keyed, value, attended, pushed, log_total, cosine, sine, scale_row,
        at_col, at_row,
    )


def chunks_of(total):
    return [(start, min(256, total - start)) for start in range(0, total, 256)]


def middle_kernel(
    experts, hidden, weights, chosen, spread, back, act_out, grad_out, strengths
):
    total = act_out.shape[1]
    rows = hidden[...]
    lane = lax.broadcasted_iota(jnp.int32, (rows.shape[0], 128), 1)
    logits = mm_nt(rows, weights[2 * total :, :])
    sigma = jax.nn.sigmoid(logits)
    masked = jnp.where((lane >= 1) & (lane <= experts), logits, NEG)
    lifted = jnp.exp(masked - jnp.max(masked, axis=1, keepdims=True))
    normal = lifted / jnp.sum(lifted, axis=1, keepdims=True)
    named = chosen[...].astype(WIDE)
    strength = jnp.where(lane == 0, sigma, normal * named)
    high = strength.astype(LOW)
    rest = (strength - high.astype(WIDE)).astype(LOW)
    strengths[...] = jnp.zeros_like(strengths)
    for start, size in chunks_of(total):
        here = pl.ds(start, size)
        gate = mm_nt(rows, weights[start : start + size, :])
        up = mm_nt(rows, weights[total + start : total + start + size, :])
        wide = mm(high, spread[:, here]) + mm(rest, spread[:, here])
        pushed = back[:, here].astype(WIDE)
        curve = jax.nn.sigmoid(gate)
        silu = gate * curve
        act = silu * up
        act_out[:, here] = (wide * act).astype(LOW)
        strengths[...] += mm_nt((act * pushed).astype(LOW), spread[:, here])
        pushed = wide * pushed
        grad_out[:, here] = (pushed * up * (curve + silu * (1.0 - curve))).astype(LOW)
        grad_out[:, pl.ds(total + start, size)] = (pushed * silu).astype(LOW)
    backs = strengths[...]
    gates_back = jnp.where(lane >= 1, backs * named, 0.0)
    logit_grad = normal * (gates_back - jnp.sum(normal * gates_back, axis=1, keepdims=True))
    logit_grad = jnp.where(lane == 0, backs * sigma * (1.0 - sigma), logit_grad)
    grad_out[:, 2 * total :] = logit_grad.astype(LOW)


def middle(hidden, weights, chosen, spread, back, experts):
    group, width = hidden.shape
    total = back.shape[1]
    rows = group // 5
    by_rows = lambda columns: pl.BlockSpec((rows, columns), lambda i: (i, 0))
    held = lambda shape: pl.BlockSpec(shape, lambda i: (0, 0), pipeline_mode=pl.Buffered(1))
    return pl.pallas_call(
        functools.partial(middle_kernel, experts),
        grid=(group // rows,),
        in_specs=[
            by_rows(width),
            held(weights.shape),
            by_rows(128),
            held(spread.shape),
            by_rows(total),
        ],
        out_specs=[by_rows(total), by_rows(weights.shape[0])],
        out_shape=[
            jax.ShapeDtypeStruct((group, total), LOW),
            jax.ShapeDtypeStruct((group, weights.shape[0]), LOW),
        ],
        scratch_shapes=[pltpu.VMEM((rows, 128), WIDE)],
        cost_estimate=work(55),
        compiler_params=pltpu.CompilerParams(vmem_limit_bytes=58 * 2**20),
    )(hidden, weights, chosen, spread, back)


def ring_blocks(block, devices, first, last):
    ring = [(i, (i + 2) % devices) for i in range(devices)]
    blocks = [block]
    for _ in range(first, last):
        blocks.append(lax.ppermute(blocks[-1], "fsdp", ring))
    return blocks


def ring_place(blocks, devices):
    mine = lax.axis_index("fsdp")
    twin = [(i, i ^ 1) for i in range(devices)]
    whole = jnp.zeros((devices,) + blocks[0].shape, blocks[0].dtype)
    for step, block in enumerate(blocks):
        owner = lax.rem(mine + devices - 2 * step, devices)
        whole = lax.dynamic_update_index_in_dim(whole, block, owner, 0)
        other = lax.ppermute(block, "fsdp", twin)
        whole = lax.dynamic_update_index_in_dim(whole, other, owner ^ 1, 0)
    return whole


def remote(source, target, sent, arrived, where):
    return pltpu.make_async_remote_copy(
        src_ref=source,
        dst_ref=target,
        send_sem=sent,
        recv_sem=arrived,
        device_id=where,
        device_id_type=pl.DeviceIdType.MESH,
    )


def open_kernel(peers):
    barrier = pltpu.get_barrier_semaphore()
    for peer in peers:
        pl.semaphore_signal(
            barrier, inc=1, device_id=peer, device_id_type=pl.DeviceIdType.MESH
        )
    pl.semaphore_wait(barrier, len(peers))


def gather_kernel(
    devices,
    reps,
    token,
    strip,
    share,
    small,
    token_all,
    strip_all,
    share_all,
    small_all,
    ring_sent,
    ring_got,
    twin_sent,
    twin_got,
    deal_sent,
    deal_got,
    rep_sent,
    rep_got,
    share_sent,
    share_got,
    pass_sent,
    pass_got,
    local_done,
):
    mine = lax.axis_index("fsdp")
    copy = lax.axis_index("rep")
    steps = devices // 2
    right = lax.rem(mine + 2, devices)
    twin = mine + 1 - 2 * lax.rem(mine, 2)
    around = [{"fsdp": lax.rem(mine + k, devices)} for k in range(1, devices)]
    across = [{"rep": lax.rem(copy + k, reps)} for k in range(1, reps)]
    open_kernel(around + across)

    owners = [lax.rem(mine + devices - 2 * s, devices) for s in range(steps)]
    inputs = (token, share, small)
    whole = (token_all, share_all.at[:, copy], small_all)
    everything = []

    def begin(one):
        one.start()
        everything.append(one)
        return one

    locals_ = [
        pltpu.make_async_copy(token, token_all.at[mine], local_done.at[0]),
        pltpu.make_async_copy(share, share_all.at[mine, copy], local_done.at[1]),
        pltpu.make_async_copy(small, small_all.at[mine], local_done.at[2]),
        pltpu.make_async_copy(strip.at[mine], strip_all.at[mine, copy], local_done.at[3]),
    ]
    def ring_step(j, s):
        source = inputs[j] if s == 0 else whole[j].at[owners[s]]
        if s + 1 < steps:
            begin(
                remote(
                    source,
                    whole[j].at[owners[s]],
                    ring_sent.at[j, s],
                    ring_got.at[j, s],
                    {"fsdp": right},
                )
            )
        begin(
            remote(
                source,
                whole[j].at[owners[s]],
                twin_sent.at[j, s],
                twin_got.at[j, s],
                {"fsdp": twin},
            )
        )

    def ring_wait(j, s):
        remote(
            inputs[j],
            whole[j].at[owners[s + 1]],
            ring_sent.at[j, s],
            ring_got.at[j, s],
            {"fsdp": right},
        ).wait_recv()

    deals = []
    for k in range(1, devices):
        peer = lax.rem(mine + k, devices)
        deals.append(
            begin(
                remote(
                    strip.at[peer],
                    strip_all.at[mine, copy],
                    deal_sent.at[k - 1],
                    deal_got.at[k - 1],
                    {"fsdp": peer},
                )
            )
        )
    ring_step(1, 0)
    ring_step(2, 0)
    ring_step(0, 0)
    for one in locals_:
        one.start()
    for s in range(1, steps):
        for j in (1, 2):
            ring_wait(j, s - 1)
            ring_step(j, s)

    if steps > 1:
        ring_wait(0, 0)
        ring_step(0, 1)
    locals_[3].wait()
    for one in deals:
        one.wait_recv()
    crossed = []
    for k in range(1, reps):
        crossed.append(
            begin(
                remote(
                    strip_all.at[:, copy],
                    strip_all.at[:, copy],
                    rep_sent.at[k - 1],
                    rep_got.at[k - 1],
                    {"rep": lax.rem(copy + k, reps)},
                )
            )
        )
    shared = []
    for k in range(1, reps):
        for s in range(steps):
            source = share if s == 0 else share_all.at[owners[s], copy]
            shared.append(
                begin(
                    remote(
                        source,
                        share_all.at[owners[s], copy],
                        share_sent.at[k - 1, s],
                        share_got.at[k - 1, s],
                        {"rep": lax.rem(copy + k, reps)},
                    )
                )
            )
    if steps > 2:
        ring_wait(0, 1)
        ring_step(0, 2)
    for k in range(1, reps):
        origin = lax.rem(copy + reps - k, reps)
        for s in range(steps):
            shared[(k - 1) * steps + s].wait_recv()
            begin(
                remote(
                    share_all.at[owners[s], origin],
                    share_all.at[owners[s], origin],
                    pass_sent.at[k - 1, s],
                    pass_got.at[k - 1, s],
                    {"fsdp": twin},
                )
            )
    for s in range(3, steps):
        ring_wait(0, s - 1)
        ring_step(0, s)
    for one in everything:
        one.wait_send()
    for j in range(3):
        for s in range(steps):
            remote(
                inputs[j],
                whole[j].at[owners[s]],
                twin_sent.at[j, s],
                twin_got.at[j, s],
                {"fsdp": twin},
            ).wait_recv()
    for one in crossed:
        one.wait_recv()
    for k in range(1, reps):
        for s in range(steps):
            remote(
                share,
                share_all.at[owners[s], copy],
                pass_sent.at[k - 1, s],
                pass_got.at[k - 1, s],
                {"fsdp": twin},
            ).wait_recv()
    for one in locals_[:3]:
        one.wait()


def gather_all(token, strip, share, small, reps):
    devices, piece, columns = strip.shape
    steps = devices // 2
    dma = pltpu.SemaphoreType.DMA
    anywhere = pl.BlockSpec(memory_space=pl.ANY)
    return pl.pallas_call(
        functools.partial(gather_kernel, devices, reps),
        in_specs=[pl.BlockSpec(memory_space=pltpu.VMEM)] * 4,
        out_specs=[anywhere] * 4,
        out_shape=[
            jax.ShapeDtypeStruct((devices,) + token.shape, LOW),
            jax.ShapeDtypeStruct((devices, reps, piece, columns), LOW),
            jax.ShapeDtypeStruct((devices, reps) + share.shape, LOW),
            jax.ShapeDtypeStruct((devices,) + small.shape, LOW),
        ],
        scratch_shapes=[
            dma((3, steps)),
            dma((3, steps)),
            dma((3, steps)),
            dma((3, steps)),
            dma((devices - 1,)),
            dma((devices - 1,)),
            dma((reps - 1,)),
            dma((reps - 1,)),
            dma((reps - 1, steps)),
            dma((reps - 1, steps)),
            dma((reps - 1, steps)),
            dma((reps - 1, steps)),
            dma((4,)),
        ],
        cost_estimate=work(100),
        compiler_params=pltpu.CompilerParams(collective_id=0, has_side_effects=True),
    )(token, strip, share, small)


def reduce_rep(values):
    return lax.psum(values, "rep")


def shards(
    tokens,
    lengths,
    dealing,
    routes,
    cotangent,
    first_gain,
    projection,
    projection_bias,
    output_weight,
    second_gain,
    router_weight,
    shared_gate,
    shared_in,
    shared_out,
    expert_in,
    expert_out,
):
    width = tokens.shape[1]
    rows = tokens.shape[0]
    group = dealing.shape[0]
    devices = group // rows
    part = width // devices
    held = part // HEAD_DIM
    experts, _, _, units = expert_in.shape
    hidden = -(-units // 16) * 16
    common = shared_out.shape[0]
    total = common + experts * hidden
    reps = lax.axis_size("rep")
    piece = part // reps
    mine = lax.axis_index("fsdp")
    copy = lax.axis_index("rep")
    scale = HEAD_DIM ** (-0.5)

    gain_one = first_gain.astype(WIDE)
    strip = lax.dynamic_slice_in_dim(projection, copy * piece, piece, 0).astype(WIDE)
    strip = (lax.dynamic_slice_in_dim(gain_one, copy * piece, piece, 0)[:, None] * strip).astype(LOW)
    strip = strip.reshape(piece, 3, devices, part).transpose(2, 0, 1, 3)
    strip = strip.reshape(devices, piece, 3 * part)
    share = lax.dynamic_slice_in_dim(output_weight, copy * piece, piece, 0)
    small = jnp.concatenate(
        [second_gain, shared_gate, projection_bias, router_weight.reshape(-1)]
    )
    length = small.shape[0]
    small = jnp.pad(small, (0, -length % 2048)).reshape(-1, 128)
    token_all, strip, share, small = gather_all(tokens, strip, share, small, reps)
    token_all = token_all.reshape(group, width)
    weight_mine = strip.reshape(width, 3 * part)
    weight_output = share.reshape(width, width)
    small = small.reshape(devices, -1)[:, :length]
    cot_in, _ = lax.optimization_barrier((cotangent, token_all))
    steps = devices // 2
    cot_blocks = ring_blocks(cot_in, devices, 0, steps // 2)

    gain_two = small[:, :part].reshape(width).astype(WIDE)
    gate_weight = small[:, part : 2 * part].reshape(width, 1)
    bias = small[:, 2 * part : 5 * part].reshape(3, devices, part)
    bias_mine = lax.dynamic_slice_in_dim(bias, mine, 1, 1).reshape(3 * part).astype(WIDE)
    router = small[:, 5 * part :].reshape(width, experts)
    choice_weight = jnp.concatenate(
        [gate_weight, router, jnp.zeros((width, 127 - experts), LOW)], axis=1
    )
    full = -(-total // 128) * 128
    expert_rows = expert_in.transpose(0, 1, 3, 2)
    expert_down = expert_out
    if hidden > units:
        expert_rows = jnp.pad(expert_rows, ((0, 0), (0, 0), (0, hidden - units), (0, 0)))
        expert_down = jnp.pad(expert_down, ((0, 0), (0, hidden - units), (0, 0)))
    fill = jnp.zeros((full - total, width), LOW)
    weights = []
    for half in range(2):
        weights.append(shared_in[half].T)
        weights.append(expert_rows[:, half].reshape(experts * hidden, width))
        weights.append(fill)
    weights = jnp.concatenate(weights + [choice_weight.T], axis=0)
    weight_down = jnp.concatenate(
        [shared_out, expert_down.reshape(experts * hidden, width), fill], axis=0
    )

    scale_all = scale_of(token_all.astype(WIDE))
    projected = scale_all * mm(token_all, weight_mine) + bias_mine
    first_length = lengths[0, 0]
    second = (dealing >= first_length).astype(jnp.int32)
    cosine, sine = rope_tables(dealing - second * first_length)
    shape = (devices, rows, HEAD_DIM)
    cosine = jnp.concatenate([cosine, cosine], axis=1).reshape(shape)
    sine = jnp.concatenate([-sine, sine], axis=1).reshape(shape)
    size = 256 // devices
    at_col = jnp.broadcast_to(dealing.reshape(devices, rows, 1), shape)
    at_row = dealing.reshape(devices, rows // size, size).transpose(1, 0, 2)
    at_row = at_row.reshape(rows // size, 1, devices * size)
    scale_row = jnp.broadcast_to(scale_all.reshape(devices, rows, 1), shape)
    query, keyed, value, attended_mine, log_total = attend(
        lengths[0], projected.reshape(devices, rows, 3 * part), cosine, sine, at_col, at_row,
        held, size,
    )
    attended, halfway = lax.optimization_barrier(
        (attended_mine.reshape(group, part), cot_blocks[-1])
    )
    cot_blocks = cot_blocks[:-1] + ring_blocks(halfway, devices, steps // 2, steps - 1)
    cot_all = ring_place(cot_blocks, devices).reshape(group, width)
    attended = lax.all_to_all(attended, "fsdp", split_axis=0, concat_axis=1, tiled=True)

    residual = tokens.astype(WIDE) + mm(attended, weight_output)
    scale_two = scale_of(residual)
    unit = residual * scale_two
    hidden_two = (unit * gain_two).astype(LOW)
    hidden_blocks = ring_blocks(hidden_two, devices, 0, steps - 1)
    hidden_all = ring_place(hidden_blocks, devices).reshape(group, width)

    lane = jnp.arange(128, dtype=jnp.int32)
    chosen = jnp.any(routes[:, :, None] + 1 == lane[None, None, :], axis=1).astype(LOW)
    owner = jnp.concatenate(
        [
            jnp.zeros((common,), jnp.int32),
            1 + jnp.repeat(jnp.arange(experts, dtype=jnp.int32), hidden),
            jnp.full((full - total,), 127, jnp.int32),
        ]
    )
    spread = (owner[None, :] == lane[:, None]).astype(LOW)
    back = mm_nt(cot_all, weight_down, LOW)
    act_low, grads = middle(hidden_all, weights, chosen, spread, back, experts)

    down_grad = mm_tn(act_low, cot_all, LOW)
    in_grad = mm_tn(grads, hidden_all, LOW)
    choice_weight_grad = in_grad[2 * full :].T
    grads, down_grad, in_grad = lax.optimization_barrier((grads, down_grad, in_grad))
    down_grad = reduce_rep(down_grad)
    hidden_back = mm(grads, weights, LOW)
    act_low, in_grad, hidden_back = lax.optimization_barrier((act_low, in_grad, hidden_back))
    in_grad, down_grad = lax.optimization_barrier((in_grad, down_grad))
    in_grad = reduce_rep(in_grad)
    hidden_back = lax.psum_scatter(hidden_back, "fsdp", scatter_dimension=0, tiled=True)
    hidden_back = hidden_back.astype(WIDE)
    layered = mm(act_low, weight_down, LOW)

    gain_two_grad = jnp.sum(hidden_back * unit, axis=0)
    pushed = hidden_back * gain_two
    residual_grad = cotangent.astype(WIDE) + scale_two * (
        pushed - unit * jnp.mean(pushed * unit, axis=-1, keepdims=True)
    )
    output_low = residual_grad.astype(LOW)
    attended_back = mm_nt(output_low, weight_output, LOW)
    attended_back = lax.all_to_all(
        attended_back, "fsdp", split_axis=1, concat_axis=0, tiled=True
    ).reshape(devices, rows, part)
    attended_back, attended_held = lax.optimization_barrier((attended_back, attended))
    lane = jnp.arange(128, dtype=jnp.int32)
    extra = jnp.where(
        lane[None, :] == experts + 1, gain_two_grad[:, None].astype(LOW), choice_weight_grad
    )
    output_grad = jnp.concatenate([mm_tn(attended_held, output_low, LOW), extra], axis=1)
    layered, output_grad = lax.optimization_barrier((layered, output_grad))
    layered = lax.psum_scatter(layered, "fsdp", scatter_dimension=0, tiled=True)
    mixed = (residual + layered.astype(WIDE)).astype(LOW)
    output_grad = lax.psum_scatter(output_grad, "fsdp", scatter_dimension=0, tiled=True)

    parts = attend_back(
        lengths[0], query, keyed, value, attended_mine, attended_back, log_total, cosine, sine,
        scale_row, at_col, at_row, held, size,
    )
    projected_back = jnp.concatenate(parts[:3], axis=2).reshape(group, 3 * part)
    scaled_back = jnp.concatenate(parts[3:], axis=2).reshape(group, 3 * part)
    bias_grad = jnp.sum(projected_back.astype(WIDE), axis=0)
    weight_grad = mm_tn(token_all, scaled_back, LOW)
    bias_rows = jnp.broadcast_to(
        bias_grad.astype(LOW).reshape(1, 1, 3, part), (devices, 16, 3, part)
    )
    weight_grad = jnp.concatenate([weight_grad.reshape(devices, part, 3, part), bias_rows], axis=1)
    weight_grad = lax.all_to_all(
        weight_grad, "fsdp", split_axis=0, concat_axis=2, tiled=False
    ).reshape(part + 16, 3 * width)
    weight_grad, projected_back = lax.optimization_barrier((weight_grad, projected_back))
    token_back = mm_nt(projected_back, weight_mine, LOW)
    weight_grad, _ = lax.optimization_barrier((weight_grad, token_back))
    weight_grad, output_grad, in_grad, down_grad = lax.optimization_barrier(
        (weight_grad, output_grad, in_grad, down_grad)
    )
    weight_grad, output_grad = lax.psum((weight_grad, output_grad), "rep")
    bias_grad = weight_grad[part].astype(WIDE).reshape(devices, 3 * part)
    bias_grad = lax.dynamic_slice_in_dim(bias_grad, mine, 1, 0)[0]
    weight_grad = weight_grad[:part].astype(WIDE)
    small = output_grad[:, width:].astype(WIDE)
    output_grad = output_grad[:, :width].astype(WIDE)
    first_gain_grad = jnp.sum(weight_grad * projection.astype(WIDE), axis=1)
    projection_grad = weight_grad * gain_one[:, None]

    pushed = lax.psum_scatter(token_back, "fsdp", scatter_dimension=0, tiled=True).astype(WIDE)
    inputs = tokens.astype(WIDE)
    scale_one = scale_of(inputs)
    unit_one = inputs * scale_one
    tokens_grad = residual_grad + scale_one * (
        pushed - unit_one * jnp.mean(pushed * unit_one, axis=-1, keepdims=True)
    )

    in_grad = in_grad[: 2 * full].reshape(2, full, width)
    shared_in_grad = in_grad[:, :common].astype(WIDE).transpose(0, 2, 1)
    expert_in_grad = in_grad[:, common:total].reshape(2, experts, hidden, width)
    expert_in_grad = expert_in_grad[:, :, :units].astype(WIDE).transpose(1, 0, 3, 2)
    down_grad = down_grad.astype(WIDE)
    return (
        mixed,
        tokens_grad,
        first_gain_grad,
        projection_grad,
        bias_grad,
        output_grad,
        small[:, experts + 1],
        small[:, 1 : experts + 1],
        small[:, 0],
        shared_in_grad,
        down_grad[:common],
        expert_in_grad,
        down_grad[common:total].reshape(experts, hidden, width)[:, :units],
    )


def solution(mesh):
    in_specs = (
        P(("rep", "fsdp"), None),
        P("rep", None),
        P("rep"),
        P("rep", None),
        P(("rep", "fsdp"), None),
        P("fsdp"),
        P("fsdp", None),
        P("fsdp"),
        P("fsdp", None),
        P("fsdp"),
        P("fsdp", None),
        P("fsdp"),
        P(None, None, "fsdp"),
        P("fsdp", None),
        P(None, None, None, "fsdp"),
        P(None, "fsdp", None),
    )
    out_specs = (
        P(("rep", "fsdp"), None),
        P(("rep", "fsdp"), None),
        P("fsdp"),
        P("fsdp", None),
        P("fsdp"),
        P("fsdp", None),
        P("fsdp"),
        P("fsdp", None),
        P("fsdp"),
        P(None, None, "fsdp"),
        P("fsdp", None),
        P(None, None, None, "fsdp"),
        P(None, "fsdp", None),
    )
    return jax.shard_map(shards, mesh=mesh, in_specs=in_specs, out_specs=out_specs, check_vma=False)
```

```python
import functools

import jax
import jax.numpy as jnp
from jax import lax
from jax.experimental import pallas as pl
from jax.experimental.pallas import tpu as pltpu
from jax.sharding import PartitionSpec as P

HEAD_DIM = 128
EPS = 1e-06
THETA = 1000000.0
NEG = -1e30
LOW = jnp.bfloat16
WIDE = jnp.float32


def dot(left, right, dims, kind=WIDE):
    return lax.dot_general(left, right, ((dims[0], dims[1]), ((), ())), preferred_element_type=kind)


def mm(left, right, kind=WIDE):
    return dot(left, right, ((1,), (0,)), kind)


def mm_nt(left, right, kind=WIDE):
    return dot(left, right, ((1,), (1,)), kind)


def mm_tn(left, right, kind=WIDE):
    return dot(left, right, ((0,), (0,)), kind)


def scale_of(values):
    return lax.rsqrt(jnp.mean(values * values, axis=-1, keepdims=True) + EPS)


def rope_tables(position):
    half = HEAD_DIM // 2
    freq = THETA ** (-(jnp.arange(half, dtype=WIDE) * (2.0 / HEAD_DIM)))
    angle = position.astype(WIDE)[:, None] * freq[None, :]
    return (jnp.cos(angle), jnp.sin(angle))


def pair_block(ref, index, size, head=0):
    block = ref[
        :,
        pl.ds(pl.multiple_of(index * size, size), size),
        head * HEAD_DIM : (head + 1) * HEAD_DIM,
    ]
    return block.reshape(block.shape[0] * size, HEAD_DIM)


def put_block(ref, index, size, block, head=0):
    ref[
        :,
        pl.ds(pl.multiple_of(index * size, size), size),
        head * HEAD_DIM : (head + 1) * HEAD_DIM,
    ] = block.reshape(ref.shape[0], size, HEAD_DIM)


def first_block(first_length, index, width):
    return jnp.where(index * width >= first_length, first_length // width, 0)


def span_mask(at_col, at_row, first_length):
    lowest = jnp.where(at_col >= first_length, first_length, 0)
    return (at_row <= at_col) & (at_row >= lowest)


def attend_kernel(
    size,
    held,
    lengths,
    projected,
    cosine,
    sine,
    at_col,
    at_row,
    query,
    keyed,
    value,
    out,
    log_total,
):
    devices, rows, _ = projected.shape
    width = size * devices
    first_length = lengths[0]
    factor = HEAD_DIM ** (-0.5)

    def prepare(index, carry):
        wave, ripple = pair_block(cosine, index, size), pair_block(sine, index, size)
        for head in range(held):
            for place, target in ((0, query), (held, keyed)):
                block = pair_block(projected, index, size, place + head)
                block = block * wave + pltpu.roll(block, HEAD_DIM // 2, 1) * ripple
                put_block(target, index, size, block.astype(LOW), head)
            block = pair_block(projected, index, size, 2 * held + head)
            put_block(value, index, size, block.astype(LOW), head)
        return carry

    lax.fori_loop(0, rows // size, prepare, 0)

    def for_queries(index, carry):
        blocks = [pair_block(query, index, size, head) for head in range(held)]
        places = pair_block(at_col, index, size)[:, :1]

        def for_keys(other, states):
            seen = span_mask(places, at_row[other], first_length)
            out_states = []
            for head, (peak, total, summed) in enumerate(states):
                raw = mm_nt(blocks[head], pair_block(keyed, other, size, head)) * factor
                raw = jnp.where(seen, raw, NEG)
                higher = jnp.maximum(peak, jnp.max(raw, axis=1, keepdims=True))
                lifted = jnp.exp(raw - higher)
                fade = jnp.exp(peak - higher)
                total = total * fade + jnp.sum(lifted, axis=1, keepdims=True)
                summed = summed * fade + mm(
                    lifted.astype(LOW), pair_block(value, other, size, head)
                )
                out_states.append((higher, total, summed))
            return tuple(out_states)

        start = (
            jnp.full((width, 1), 2 * NEG, WIDE),
            jnp.zeros((width, 1), WIDE),
            jnp.zeros((width, HEAD_DIM), WIDE),
        )
        lowest = first_block(first_length, index, width)
        states = lax.fori_loop(lowest, index + 1, for_keys, (start,) * held)
        for head, (peak, total, summed) in enumerate(states):
            put_block(out, index, size, (summed / total).astype(LOW), head)
            logs = jnp.broadcast_to(peak + jnp.log(total), (width, HEAD_DIM))
            put_block(log_total, index, size, logs, head)
        return carry

    lax.fori_loop(0, rows // size, for_queries, 0)


def attend_back_kernel(
    size,
    held,
    lengths,
    query,
    keyed,
    value,
    attended,
    attended_back,
    log_total,
    cosine,
    sine,
    scale_row,
    at_col,
    at_row,
    projected_back,
    scaled_back,
    query_sum,
    key_sum,
    value_sum,
):
    devices, rows, _ = query.shape
    width = size * devices
    first_length = lengths[0]
    factor = HEAD_DIM ** (-0.5)
    key_sum[...] = jnp.zeros_like(key_sum)
    value_sum[...] = jnp.zeros_like(value_sum)

    def for_queries(index, carry):
        places = pair_block(at_col, index, size)[:, :1]
        held_now = []
        for head in range(held):
            pushed = pair_block(attended_back, index, size, head)
            row_dot = jnp.sum(
                pushed.astype(WIDE) * pair_block(attended, index, size, head).astype(WIDE),
                axis=1,
                keepdims=True,
            )
            logs = pair_block(log_total, index, size, head)[:, :1]
            held_now.append((pair_block(query, index, size, head), pushed, row_dot, logs))

        def for_keys(other, sums):
            seen = span_mask(places, at_row[other], first_length)
            here = pl.ds(pl.multiple_of(other * width, width), width)
            out_sums = []
            for head, (block, pushed, row_dot, logs) in enumerate(held_now):
                key_block = pair_block(keyed, other, size, head)
                raw = jnp.where(seen, mm_nt(block, key_block) * factor, NEG)
                probs = jnp.exp(raw - logs)
                prob_back = mm_nt(pushed, pair_block(value, other, size, head))
                score_back = (probs * (prob_back - row_dot)).astype(LOW)
                value_sum[head, here, :] += mm_tn(probs.astype(LOW), pushed)
                key_sum[head, here, :] += mm_tn(score_back, block)
                out_sums.append(sums[head] + mm(score_back, key_block))
            return tuple(out_sums)

        lowest = first_block(first_length, index, width)
        start = (jnp.zeros((width, HEAD_DIM), WIDE),) * held
        sums = lax.fori_loop(lowest, index + 1, for_keys, start)
        here = pl.ds(pl.multiple_of(index * width, width), width)
        for head in range(held):
            query_sum[head, here, :] = sums[head]
        return carry

    lax.fori_loop(0, rows // size, for_queries, 0)

    def finish(index, carry):
        wave, ripple = pair_block(cosine, index, size), pair_block(sine, index, size)
        scale = pair_block(scale_row, index, size)[:, :1]
        here = pl.ds(pl.multiple_of(index * width, width), width)
        for head in range(held):
            for place, source in ((0, query_sum), (held, key_sum)):
                block = source[head, here, :] * factor
                block = block * wave - pltpu.roll(block, HEAD_DIM // 2, 1) * ripple
                block = block.astype(LOW)
                put_block(projected_back, index, size, block, place + head)
                put_block(
                    scaled_back, index, size, (block.astype(WIDE) * scale).astype(LOW), place + head
                )
            block = value_sum[head, here, :].astype(LOW)
            put_block(projected_back, index, size, block, 2 * held + head)
            block = (block.astype(WIDE) * scale).astype(LOW)
            put_block(scaled_back, index, size, block, 2 * held + head)
        return carry

    lax.fori_loop(0, rows // size, finish, 0)


def attend(lengths, projected, cosine, sine, at_col, at_row, held, size):
    devices, rows, _ = projected.shape
    low = jax.ShapeDtypeStruct((devices, rows, held * HEAD_DIM), LOW)
    inside = pl.BlockSpec(memory_space=pltpu.VMEM)
    return pl.pallas_call(
        functools.partial(attend_kernel, size, held),
        in_specs=[pl.BlockSpec(memory_space=pltpu.SMEM)] + [inside] * 5,
        out_specs=[inside] * 5,
        out_shape=[low] * 4 + [jax.ShapeDtypeStruct(low.shape, WIDE)],
        cost_estimate=work(30),
        compiler_params=pltpu.CompilerParams(vmem_limit_bytes=56 * 2**20),
    )(lengths, projected, cosine, sine, at_col, at_row)


def attend_back(
    lengths, query, keyed, value, attended, pushed, log_total, cosine, sine, scale_row,
    at_col, at_row, held, size,
):
    devices, rows, _ = query.shape
    low = jax.ShapeDtypeStruct((devices, rows, 3 * held * HEAD_DIM), LOW)
    inside = pl.BlockSpec(memory_space=pltpu.VMEM)
    return pl.pallas_call(
        functools.partial(attend_back_kernel, size, held),
        in_specs=[pl.BlockSpec(memory_space=pltpu.SMEM)] + [inside] * 11,
        out_specs=[inside] * 2,
        out_shape=[low] * 2,
        cost_estimate=work(1),
        scratch_shapes=[pltpu.VMEM((held, devices * rows, HEAD_DIM), WIDE)] * 3,
        compiler_params=pltpu.CompilerParams(vmem_limit_bytes=56 * 2**20),
    )(
        lengths, query, keyed, value, attended, pushed, log_total, cosine, sine, scale_row,
        at_col, at_row,
    )


def work(micros):
    return pl.CostEstimate(
        flops=int(micros * 1e9), bytes_accessed=int(micros * 3e6), transcendentals=0
    )


def chunks_of(total):
    return [(start, min(256, total - start)) for start in range(0, total, 256)]


def ring_blocks(block, devices, first, last):
    ring = [(i, (i + 2) % devices) for i in range(devices)]
    blocks = [block]
    for _ in range(first, last):
        blocks.append(lax.ppermute(blocks[-1], "fsdp", ring))
    return blocks


def ring_place(blocks, devices):
    mine = lax.axis_index("fsdp")
    twin = [(i, i ^ 1) for i in range(devices)]
    whole = jnp.zeros((devices,) + blocks[0].shape, blocks[0].dtype)
    for step, block in enumerate(blocks):
        owner = lax.rem(mine + devices - 2 * step, devices)
        whole = lax.dynamic_update_index_in_dim(whole, block, owner, 0)
        other = lax.ppermute(block, "fsdp", twin)
        whole = lax.dynamic_update_index_in_dim(whole, other, owner ^ 1, 0)
    return whole


def remote(source, target, sent, arrived, where):
    return pltpu.make_async_remote_copy(
        src_ref=source,
        dst_ref=target,
        send_sem=sent,
        recv_sem=arrived,
        device_id=where,
        device_id_type=pl.DeviceIdType.MESH,
    )


def open_kernel(peers):
    barrier = pltpu.get_barrier_semaphore()
    for peer in peers:
        pl.semaphore_signal(
            barrier, inc=1, device_id=peer, device_id_type=pl.DeviceIdType.MESH
        )
    pl.semaphore_wait(barrier, len(peers))


def middle_block(experts, rows, cot, weights, weight_down, named, spread, act_out, grad_out, strengths):
    total = act_out.shape[1]
    lane = lax.broadcasted_iota(jnp.int32, (rows.shape[0], 128), 1)
    logits = mm_nt(rows, weights[2 * total :, :])
    sigma = jax.nn.sigmoid(logits)
    masked = jnp.where((lane >= 1) & (lane <= experts), logits, NEG)
    lifted = jnp.exp(masked - jnp.max(masked, axis=1, keepdims=True))
    normal = lifted / jnp.sum(lifted, axis=1, keepdims=True)
    strength = jnp.where(lane == 0, sigma, normal * named)
    high = strength.astype(LOW)
    rest = (strength - high.astype(WIDE)).astype(LOW)
    strengths[...] = jnp.zeros_like(strengths)
    for start, size in chunks_of(total):
        here = pl.ds(start, size)
        gate = mm_nt(rows, weights[start : start + size, :])
        up = mm_nt(rows, weights[total + start : total + start + size, :])
        pushed = mm_nt(cot, weight_down[start : start + size, :])
        wide = mm(high, spread[:, here]) + mm(rest, spread[:, here])
        curve = jax.nn.sigmoid(gate)
        silu = gate * curve
        act = silu * up
        act_out[:, here] = (wide * act).astype(LOW)
        strengths[...] += mm_nt((act * pushed).astype(LOW), spread[:, here])
        pushed = wide * pushed
        grad_out[:, here] = (pushed * up * (curve + silu * (1.0 - curve))).astype(LOW)
        grad_out[:, pl.ds(total + start, size)] = (pushed * silu).astype(LOW)
    backs = strengths[...]
    gates_back = jnp.where(lane >= 1, backs * named, 0.0)
    logit_grad = normal * (gates_back - jnp.sum(normal * gates_back, axis=1, keepdims=True))
    logit_grad = jnp.where(lane == 0, backs * sigma * (1.0 - sigma), logit_grad)
    grad_out[:, 2 * total :] = logit_grad.astype(LOW)


def middle_kernel(
    devices,
    experts,
    hidden,
    cot_all,
    weights_far,
    down_far,
    chosen,
    spread,
    hidden_all,
    act_all,
    grad_all,
    weights,
    weight_down,
    strengths,
    ring_sent,
    ring_got,
    twin_sent,
    twin_got,
    local_done,
):
    mine = lax.axis_index("fsdp")
    steps = devices // 2
    rows, width = hidden.shape
    total = act_all.shape[2]
    right = lax.rem(mine + 2, devices)
    left = lax.rem(mine + devices - 2, devices)
    twin = mine + 1 - 2 * lax.rem(mine, 2)
    open_kernel([{"fsdp": right}, {"fsdp": left}, {"fsdp": twin}])
    loads = [
        pltpu.make_async_copy(hidden, hidden_all.at[mine], local_done.at[0]),
        pltpu.make_async_copy(weights_far, weights, local_done.at[1]),
        pltpu.make_async_copy(down_far, weight_down, local_done.at[2]),
    ]
    for one in loads:
        one.start()
    loads[0].wait()

    def along(s, where, sent, got):
        block = hidden_all.at[lax.rem(mine + devices - 2 * s, devices)]
        return remote(block, block, sent.at[s], got.at[s], {"fsdp": where})

    def body(rows_in, cot_in, named, act_out, grad_out):
        middle_block(
            experts,
            rows_in[0],
            cot_in[0],
            weights,
            weight_down,
            named[0].astype(WIDE),
            spread,
            act_out.at[0],
            grad_out.at[0],
            strengths,
        )

    def step(s, carry):
        @pl.when(s > 0)
        def _():
            along(s - 1, right, ring_sent, ring_got).wait_recv()

        @pl.when(s < steps - 1)
        def _():
            along(s, right, ring_sent, ring_got).start()

        along(s, twin, twin_sent, twin_got).start()
        along(s, twin, twin_sent, twin_got).wait_recv()

        @pl.when(s == 0)
        def _():
            loads[1].wait()
            loads[2].wait()

        first = lax.rem(mine - lax.rem(mine, 2) + devices - 2 * s, devices)
        by_rows = lambda columns: pl.BlockSpec((1, rows, columns), lambda i: (first + i, 0, 0))
        pltpu.emit_pipeline(
            body,
            grid=(2,),
            in_specs=[by_rows(width), by_rows(width), by_rows(128)],
            out_specs=[by_rows(total), by_rows(2 * total + 128)],
        )(hidden_all, cot_all, chosen, act_all, grad_all)
        return carry

    lax.fori_loop(0, steps, step, 0)
    for s in range(steps):
        if s < steps - 1:
            along(s, right, ring_sent, ring_got).wait_send()
        along(s, twin, twin_sent, twin_got).wait_send()


def middle(hidden, cot_all, weights, weight_down, chosen, spread, experts):
    devices, rows, width = cot_all.shape
    total = weight_down.shape[0]
    dma = pltpu.SemaphoreType.DMA
    anywhere = pl.BlockSpec(memory_space=pl.ANY)
    inside = pl.BlockSpec(memory_space=pltpu.VMEM)
    low = lambda columns: jax.ShapeDtypeStruct((devices, rows, columns), LOW)
    return pl.pallas_call(
        functools.partial(middle_kernel, devices, experts),
        in_specs=[inside, anywhere, anywhere, anywhere, anywhere, inside],
        out_specs=[anywhere] * 3,
        out_shape=[low(width), low(total), low(2 * total + 128)],
        scratch_shapes=[
            pltpu.VMEM(weights.shape, LOW),
            pltpu.VMEM(weight_down.shape, LOW),
            pltpu.VMEM((rows, 128), WIDE),
            dma((devices // 2,)),
            dma((devices // 2,)),
            dma((devices // 2,)),
            dma((devices // 2,)),
            dma((3,)),
        ],
        cost_estimate=work(110),
        compiler_params=pltpu.CompilerParams(
            collective_id=1, has_side_effects=True, vmem_limit_bytes=60 * 2**20
        ),
    )(hidden, cot_all, weights, weight_down, chosen, spread)


def gather_kernel(
    devices,
    reps,
    token,
    strip,
    share,
    small,
    token_all,
    strip_all,
    share_all,
    small_all,
    ring_sent,
    ring_got,
    twin_sent,
    twin_got,
    deal_sent,
    deal_got,
    rep_sent,
    rep_got,
    share_sent,
    share_got,
    pass_sent,
    pass_got,
    local_done,
):
    mine = lax.axis_index("fsdp")
    copy = lax.axis_index("rep")
    steps = devices // 2
    right = lax.rem(mine + 2, devices)
    twin = mine + 1 - 2 * lax.rem(mine, 2)
    around = [{"fsdp": lax.rem(mine + k, devices)} for k in range(1, devices)]
    across = [{"rep": lax.rem(copy + k, reps)} for k in range(1, reps)]
    open_kernel(around + across)

    owners = [lax.rem(mine + devices - 2 * s, devices) for s in range(steps)]
    inputs = (token, share, small)
    whole = (token_all, share_all.at[:, copy], small_all)
    everything = []

    def begin(one):
        one.start()
        everything.append(one)
        return one

    locals_ = [
        pltpu.make_async_copy(token, token_all.at[mine], local_done.at[0]),
        pltpu.make_async_copy(share, share_all.at[mine, copy], local_done.at[1]),
        pltpu.make_async_copy(small, small_all.at[mine], local_done.at[2]),
        pltpu.make_async_copy(strip.at[mine], strip_all.at[mine, copy], local_done.at[3]),
    ]
    def ring_step(j, s):
        source = inputs[j] if s == 0 else whole[j].at[owners[s]]
        if s + 1 < steps:
            begin(
                remote(
                    source,
                    whole[j].at[owners[s]],
                    ring_sent.at[j, s],
                    ring_got.at[j, s],
                    {"fsdp": right},
                )
            )
        begin(
            remote(
                source,
                whole[j].at[owners[s]],
                twin_sent.at[j, s],
                twin_got.at[j, s],
                {"fsdp": twin},
            )
        )

    def ring_wait(j, s):
        remote(
            inputs[j],
            whole[j].at[owners[s + 1]],
            ring_sent.at[j, s],
            ring_got.at[j, s],
            {"fsdp": right},
        ).wait_recv()

    shared = {}

    def share_cross(s):
        source = share if s == 0 else share_all.at[owners[s], copy]
        for k in range(1, reps):
            shared[k, s] = begin(
                remote(
                    source,
                    share_all.at[owners[s], copy],
                    share_sent.at[k - 1, s],
                    share_got.at[k - 1, s],
                    {"rep": lax.rem(copy + k, reps)},
                )
            )

    ring_step(1, 0)
    ring_step(2, 0)
    ring_step(0, 0)
    deals = []
    for k in range(1, devices):
        peer = lax.rem(mine + k, devices)
        deals.append(
            begin(
                remote(
                    strip.at[peer],
                    strip_all.at[mine, copy],
                    deal_sent.at[k - 1],
                    deal_got.at[k - 1],
                    {"fsdp": peer},
                )
            )
        )
    share_cross(0)
    for one in locals_:
        one.start()
    for s in range(1, steps):
        for j in (1, 2):
            ring_wait(j, s - 1)
            ring_step(j, s)
        share_cross(s)
    if steps > 1:
        ring_wait(0, 0)
        ring_step(0, 1)
    locals_[3].wait()
    for one in deals:
        one.wait_recv()
    crossed = []
    for k in range(1, reps):
        crossed.append(
            begin(
                remote(
                    strip_all.at[:, copy],
                    strip_all.at[:, copy],
                    rep_sent.at[k - 1],
                    rep_got.at[k - 1],
                    {"rep": lax.rem(copy + k, reps)},
                )
            )
        )
    if steps > 2:
        ring_wait(0, 1)
        ring_step(0, 2)
    for s in range(steps):
        for k in range(1, reps):
            origin = lax.rem(copy + reps - k, reps)
            shared[k, s].wait_recv()
            begin(
                remote(
                    share_all.at[owners[s], origin],
                    share_all.at[owners[s], origin],
                    pass_sent.at[k - 1, s],
                    pass_got.at[k - 1, s],
                    {"fsdp": twin},
                )
            )
    for s in range(3, steps):
        ring_wait(0, s - 1)
        ring_step(0, s)
    for one in everything:
        one.wait_send()
    for j in range(3):
        for s in range(steps):
            remote(
                inputs[j],
                whole[j].at[owners[s]],
                twin_sent.at[j, s],
                twin_got.at[j, s],
                {"fsdp": twin},
            ).wait_recv()
    for one in crossed:
        one.wait_recv()
    for k in range(1, reps):
        for s in range(steps):
            remote(
                share,
                share_all.at[owners[s], copy],
                pass_sent.at[k - 1, s],
                pass_got.at[k - 1, s],
                {"fsdp": twin},
            ).wait_recv()
    for one in locals_[:3]:
        one.wait()


def gather_all(token, strip, share, small, reps):
    devices, piece, columns = strip.shape
    steps = devices // 2
    dma = pltpu.SemaphoreType.DMA
    anywhere = pl.BlockSpec(memory_space=pl.ANY)
    return pl.pallas_call(
        functools.partial(gather_kernel, devices, reps),
        in_specs=[pl.BlockSpec(memory_space=pltpu.VMEM)] * 4,
        out_specs=[anywhere] * 4,
        out_shape=[
            jax.ShapeDtypeStruct((devices,) + token.shape, LOW),
            jax.ShapeDtypeStruct((devices, reps, piece, columns), LOW),
            jax.ShapeDtypeStruct((devices, reps) + share.shape, LOW),
            jax.ShapeDtypeStruct((devices,) + small.shape, LOW),
        ],
        scratch_shapes=[
            dma((3, steps)),
            dma((3, steps)),
            dma((3, steps)),
            dma((3, steps)),
            dma((devices - 1,)),
            dma((devices - 1,)),
            dma((reps - 1,)),
            dma((reps - 1,)),
            dma((reps - 1, steps)),
            dma((reps - 1, steps)),
            dma((reps - 1, steps)),
            dma((reps - 1, steps)),
            dma((4,)),
        ],
        cost_estimate=work(100),
        compiler_params=pltpu.CompilerParams(collective_id=0, has_side_effects=True),
    )(token, strip, share, small)


def reduce_rep(values):
    return lax.psum(values, "rep")


def shards(
    tokens,
    lengths,
    dealing,
    routes,
    cotangent,
    first_gain,
    projection,
    projection_bias,
    output_weight,
    second_gain,
    router_weight,
    shared_gate,
    shared_in,
    shared_out,
    expert_in,
    expert_out,
):
    width = tokens.shape[1]
    rows = tokens.shape[0]
    group = dealing.shape[0]
    devices = group // rows
    part = width // devices
    held = part // HEAD_DIM
    experts, _, _, units = expert_in.shape
    hidden = -(-units // 16) * 16
    common = shared_out.shape[0]
    total = common + experts * hidden
    reps = lax.axis_size("rep")
    piece = part // reps
    mine = lax.axis_index("fsdp")
    copy = lax.axis_index("rep")
    scale = HEAD_DIM ** (-0.5)

    gain_one = first_gain.astype(WIDE)
    strip = lax.dynamic_slice_in_dim(projection, copy * piece, piece, 0).astype(WIDE)
    strip = (lax.dynamic_slice_in_dim(gain_one, copy * piece, piece, 0)[:, None] * strip).astype(LOW)
    strip = strip.reshape(piece, 3, devices, part).transpose(2, 0, 1, 3)
    strip = strip.reshape(devices, piece, 3 * part)
    share = lax.dynamic_slice_in_dim(output_weight, copy * piece, piece, 0)
    small = jnp.concatenate(
        [second_gain, shared_gate, projection_bias, router_weight.reshape(-1)]
    )
    length = small.shape[0]
    small = jnp.pad(small, (0, -length % 2048)).reshape(-1, 128)
    token_all, strip, share, small = gather_all(tokens, strip, share, small, reps)
    token_all = token_all.reshape(group, width)
    weight_mine = strip.reshape(width, 3 * part)
    weight_output = share.reshape(width, width)
    small = small.reshape(devices, -1)[:, :length]
    cot_in, _ = lax.optimization_barrier((cotangent, token_all))
    steps = devices // 2
    cot_blocks = ring_blocks(cot_in, devices, 0, 1)

    gain_two = small[:, :part].reshape(width).astype(WIDE)
    gate_weight = small[:, part : 2 * part].reshape(width, 1)
    bias = small[:, 2 * part : 5 * part].reshape(3, devices, part)
    bias_mine = lax.dynamic_slice_in_dim(bias, mine, 1, 1).reshape(3 * part).astype(WIDE)
    router = small[:, 5 * part :].reshape(width, experts)
    choice_weight = jnp.concatenate(
        [gate_weight, router, jnp.zeros((width, 127 - experts), LOW)], axis=1
    )
    scale_all = scale_of(token_all.astype(WIDE))
    projected = scale_all * mm(token_all, weight_mine) + bias_mine
    first_length = lengths[0, 0]
    second = (dealing >= first_length).astype(jnp.int32)
    cosine, sine = rope_tables(dealing - second * first_length)
    shape = (devices, rows, HEAD_DIM)
    cosine = jnp.concatenate([cosine, cosine], axis=1).reshape(shape)
    sine = jnp.concatenate([-sine, sine], axis=1).reshape(shape)
    size = 256 // devices
    at_col = jnp.broadcast_to(dealing.reshape(devices, rows, 1), shape)
    at_row = dealing.reshape(devices, rows // size, size).transpose(1, 0, 2)
    at_row = at_row.reshape(rows // size, 1, devices * size)
    scale_row = jnp.broadcast_to(scale_all.reshape(devices, rows, 1), shape)
    projected, first_step = lax.optimization_barrier((projected, cot_blocks[1]))
    cot_blocks = [cot_blocks[0]] + ring_blocks(first_step, devices, 1, steps // 2)
    query, keyed, value, attended_mine, log_total = attend(
        lengths[0], projected.reshape(devices, rows, 3 * part), cosine, sine, at_col, at_row,
        held, size,
    )
    attended = attended_mine.reshape(group, part)
    cot_blocks = cot_blocks[:-1] + ring_blocks(cot_blocks[-1], devices, steps // 2, steps - 1)
    cot_all = ring_place(cot_blocks, devices).reshape(group, width)
    full = -(-total // 128) * 128
    shared_in, shared_out, expert_in, expert_out, _ = lax.optimization_barrier(
        (shared_in, shared_out, expert_in, expert_out, attended_mine)
    )
    expert_rows = expert_in.transpose(0, 1, 3, 2)
    expert_down = expert_out
    if hidden > units:
        expert_rows = jnp.pad(expert_rows, ((0, 0), (0, 0), (0, hidden - units), (0, 0)))
        expert_down = jnp.pad(expert_down, ((0, 0), (0, hidden - units), (0, 0)))
    fill = jnp.zeros((full - total, width), LOW)
    weights = []
    for half in range(2):
        weights.append(shared_in[half].T)
        weights.append(expert_rows[:, half].reshape(experts * hidden, width))
        weights.append(fill)
    weights = jnp.concatenate(weights + [choice_weight.T], axis=0)
    weight_down = jnp.concatenate(
        [shared_out, expert_down.reshape(experts * hidden, width), fill], axis=0
    )

    attended = lax.all_to_all(attended, "fsdp", split_axis=0, concat_axis=1, tiled=True)

    residual = tokens.astype(WIDE) + mm(attended, weight_output)
    scale_two = scale_of(residual)
    unit = residual * scale_two
    hidden_two = (unit * gain_two).astype(LOW)
    lane = jnp.arange(128, dtype=jnp.int32)
    chosen = jnp.any(routes[:, :, None] + 1 == lane[None, None, :], axis=1).astype(LOW)
    owner = jnp.concatenate(
        [
            jnp.zeros((common,), jnp.int32),
            1 + jnp.repeat(jnp.arange(experts, dtype=jnp.int32), hidden),
            jnp.full((full - total,), 127, jnp.int32),
        ]
    )
    spread = (owner[None, :] == lane[:, None]).astype(LOW)
    hidden_all, act_low, grads = middle(
        hidden_two,
        cot_all.reshape(devices, rows, width),
        weights,
        weight_down,
        chosen.reshape(devices, rows, 128),
        spread,
        experts,
    )
    hidden_all = hidden_all.reshape(group, width)
    act_low = act_low.reshape(group, full)
    grads = grads.reshape(group, 2 * full + 128)

    down_grad = mm_tn(act_low, cot_all, LOW)
    grads, down_grad = lax.optimization_barrier((grads, down_grad))
    down_grad = reduce_rep(down_grad)
    hidden_back = mm(grads, weights, LOW)
    act_low, grads, hidden_back = lax.optimization_barrier((act_low, grads, hidden_back))
    hidden_back = lax.psum_scatter(hidden_back, "fsdp", scatter_dimension=0, tiled=True)
    hidden_back = hidden_back.astype(WIDE)
    in_grad = mm_tn(grads, hidden_all, LOW)
    choice_weight_grad = in_grad[2 * full :].T
    in_grad, down_grad = lax.optimization_barrier((in_grad, down_grad))
    in_grad = reduce_rep(in_grad)
    layered = mm(act_low, weight_down, LOW)

    gain_two_grad = jnp.sum(hidden_back * unit, axis=0)
    pushed = hidden_back * gain_two
    residual_grad = cotangent.astype(WIDE) + scale_two * (
        pushed - unit * jnp.mean(pushed * unit, axis=-1, keepdims=True)
    )
    output_low = residual_grad.astype(LOW)
    attended_back = mm_nt(output_low, weight_output, LOW)
    attended_back = lax.all_to_all(
        attended_back, "fsdp", split_axis=1, concat_axis=0, tiled=True
    ).reshape(devices, rows, part)
    attended_back, attended_held = lax.optimization_barrier((attended_back, attended))
    lane = jnp.arange(128, dtype=jnp.int32)
    extra = jnp.where(
        lane[None, :] == experts + 1, gain_two_grad[:, None].astype(LOW), choice_weight_grad
    )
    output_grad = jnp.concatenate([mm_tn(attended_held, output_low, LOW), extra], axis=1)
    output_grad = lax.psum_scatter(output_grad, "fsdp", scatter_dimension=0, tiled=True)

    parts = attend_back(
        lengths[0], query, keyed, value, attended_mine, attended_back, log_total, cosine, sine,
        scale_row, at_col, at_row, held, size,
    )
    projected_back = parts[0].reshape(group, 3 * part)
    scaled_back = parts[1].reshape(group, 3 * part)
    bias_grad = jnp.sum(projected_back.astype(WIDE), axis=0)
    weight_grad = mm_tn(token_all, scaled_back, LOW)
    bias_rows = jnp.broadcast_to(
        bias_grad.astype(LOW).reshape(1, 1, 3, part), (devices, 16, 3, part)
    )
    weight_grad = jnp.concatenate([weight_grad.reshape(devices, part, 3, part), bias_rows], axis=1)
    weight_grad = lax.all_to_all(
        weight_grad, "fsdp", split_axis=0, concat_axis=2, tiled=False
    ).reshape(part + 16, 3 * width)
    weight_grad, projected_back, layered = lax.optimization_barrier(
        (weight_grad, projected_back, layered)
    )
    token_back = mm_nt(projected_back, weight_mine, LOW)
    pushed = lax.psum_scatter(token_back, "fsdp", scatter_dimension=0, tiled=True).astype(WIDE)
    output_grad, weight_grad, in_grad, down_grad, pushed = lax.optimization_barrier(
        (output_grad, weight_grad, in_grad, down_grad, pushed)
    )
    weight_grad, output_grad = reduce_rep((weight_grad, output_grad))
    layered = lax.psum_scatter(layered, "fsdp", scatter_dimension=0, tiled=True)
    mixed = (residual + layered.astype(WIDE)).astype(LOW)
    bias_grad = weight_grad[part].astype(WIDE).reshape(devices, 3 * part)
    bias_grad = lax.dynamic_slice_in_dim(bias_grad, mine, 1, 0)[0]
    weight_grad = weight_grad[:part].astype(WIDE)
    small = output_grad[:, width:].astype(WIDE)
    output_grad = output_grad[:, :width].astype(WIDE)
    first_gain_grad = jnp.sum(weight_grad * projection.astype(WIDE), axis=1)
    projection_grad = weight_grad * gain_one[:, None]

    inputs = tokens.astype(WIDE)
    scale_one = scale_of(inputs)
    unit_one = inputs * scale_one
    tokens_grad = residual_grad + scale_one * (
        pushed - unit_one * jnp.mean(pushed * unit_one, axis=-1, keepdims=True)
    )

    in_grad = in_grad[: 2 * full].reshape(2, full, width)
    shared_in_grad = in_grad[:, :common].astype(WIDE).transpose(0, 2, 1)
    expert_in_grad = in_grad[:, common:total].reshape(2, experts, hidden, width)
    expert_in_grad = expert_in_grad[:, :, :units].astype(WIDE).transpose(1, 0, 3, 2)
    down_grad = down_grad.astype(WIDE)
    return (
        mixed,
        tokens_grad,
        first_gain_grad,
        projection_grad,
        bias_grad,
        output_grad,
        small[:, experts + 1],
        small[:, 1 : experts + 1],
        small[:, 0],
        shared_in_grad,
        down_grad[:common],
        expert_in_grad,
        down_grad[common:total].reshape(experts, hidden, width)[:, :units],
    )


def solution(mesh):
    in_specs = (
        P(("rep", "fsdp"), None),
        P("rep", None),
        P("rep"),
        P("rep", None),
        P(("rep", "fsdp"), None),
        P("fsdp"),
        P("fsdp", None),
        P("fsdp"),
        P("fsdp", None),
        P("fsdp"),
        P("fsdp", None),
        P("fsdp"),
        P(None, None, "fsdp"),
        P("fsdp", None),
        P(None, None, None, "fsdp"),
        P(None, "fsdp", None),
    )
    out_specs = (
        P(("rep", "fsdp"), None),
        P(("rep", "fsdp"), None),
        P("fsdp"),
        P("fsdp", None),
        P("fsdp"),
        P("fsdp", None),
        P("fsdp"),
        P("fsdp", None),
        P("fsdp"),
        P(None, None, "fsdp"),
        P("fsdp", None),
        P(None, None, None, "fsdp"),
        P(None, "fsdp", None),
    )
    return jax.shard_map(shards, mesh=mesh, in_specs=in_specs, out_specs=out_specs, check_vma=False)
```

```python
import functools

import jax
import jax.numpy as jnp
from jax import lax
from jax.experimental import pallas as pl
from jax.experimental.pallas import tpu as pltpu
from jax.sharding import PartitionSpec as P

HEAD_DIM = 128
EPS = 1e-06
THETA = 1000000.0
NEG = -1e30
LOW = jnp.bfloat16
WIDE = jnp.float32


def dot(left, right, dims, kind=WIDE):
    return lax.dot_general(left, right, ((dims[0], dims[1]), ((), ())), preferred_element_type=kind)


def mm(left, right, kind=WIDE):
    return dot(left, right, ((1,), (0,)), kind)


def mm_nt(left, right, kind=WIDE):
    return dot(left, right, ((1,), (1,)), kind)


def mm_tn(left, right, kind=WIDE):
    return dot(left, right, ((0,), (0,)), kind)


def scale_of(values):
    return lax.rsqrt(jnp.mean(values * values, axis=-1, keepdims=True) + EPS)


def rope_tables(position):
    half = HEAD_DIM // 2
    freq = THETA ** (-(jnp.arange(half, dtype=WIDE) * (2.0 / HEAD_DIM)))
    angle = position.astype(WIDE)[:, None] * freq[None, :]
    return (jnp.cos(angle), jnp.sin(angle))


def pair_block(ref, index, size, head=0):
    block = ref[
        :,
        pl.ds(pl.multiple_of(index * size, size), size),
        head * HEAD_DIM : (head + 1) * HEAD_DIM,
    ]
    return block.reshape(block.shape[0] * size, HEAD_DIM)


def put_block(ref, index, size, block, head=0):
    ref[
        :,
        pl.ds(pl.multiple_of(index * size, size), size),
        head * HEAD_DIM : (head + 1) * HEAD_DIM,
    ] = block.reshape(ref.shape[0], size, HEAD_DIM)


def first_block(first_length, index, width):
    return jnp.where(index * width >= first_length, first_length // width, 0)


def span_mask(at_col, at_row, first_length):
    lowest = jnp.where(at_col >= first_length, first_length, 0)
    return (at_row <= at_col) & (at_row >= lowest)


def attend_kernel(
    size,
    held,
    lengths,
    projected,
    cosine,
    sine,
    at_col,
    at_row,
    query,
    keyed,
    value,
    out,
    log_total,
):
    devices, rows, _ = projected.shape
    width = size * devices
    first_length = lengths[0]
    factor = HEAD_DIM ** (-0.5)

    def prepare(index, carry):
        wave, ripple = pair_block(cosine, index, size), pair_block(sine, index, size)
        for head in range(held):
            for place, target in ((0, query), (held, keyed)):
                block = pair_block(projected, index, size, place + head)
                block = block * wave + pltpu.roll(block, HEAD_DIM // 2, 1) * ripple
                put_block(target, index, size, block.astype(LOW), head)
            block = pair_block(projected, index, size, 2 * held + head)
            put_block(value, index, size, block.astype(LOW), head)
        return carry

    lax.fori_loop(0, rows // size, prepare, 0)

    def for_queries(index, carry):
        blocks = [pair_block(query, index, size, head) for head in range(held)]
        places = pair_block(at_col, index, size)[:, :1]

        def for_keys(other, states):
            seen = span_mask(places, at_row[other], first_length)
            out_states = []
            for head, (peak, total, summed) in enumerate(states):
                raw = mm_nt(blocks[head], pair_block(keyed, other, size, head)) * factor
                raw = jnp.where(seen, raw, NEG)
                higher = jnp.maximum(peak, jnp.max(raw, axis=1, keepdims=True))
                lifted = jnp.exp(raw - higher)
                fade = jnp.exp(peak - higher)
                total = total * fade + jnp.sum(lifted, axis=1, keepdims=True)
                summed = summed * fade + mm(
                    lifted.astype(LOW), pair_block(value, other, size, head)
                )
                out_states.append((higher, total, summed))
            return tuple(out_states)

        start = (
            jnp.full((width, 1), 2 * NEG, WIDE),
            jnp.zeros((width, 1), WIDE),
            jnp.zeros((width, HEAD_DIM), WIDE),
        )
        lowest = first_block(first_length, index, width)
        states = lax.fori_loop(lowest, index + 1, for_keys, (start,) * held)
        for head, (peak, total, summed) in enumerate(states):
            put_block(out, index, size, (summed / total).astype(LOW), head)
            logs = jnp.broadcast_to(peak + jnp.log(total), (width, HEAD_DIM))
            put_block(log_total, index, size, logs, head)
        return carry

    lax.fori_loop(0, rows // size, for_queries, 0)


def attend_back_kernel(
    size,
    held,
    lengths,
    query,
    keyed,
    value,
    attended,
    attended_back,
    log_total,
    cosine,
    sine,
    scale_row,
    at_col,
    at_row,
    projected_back,
    scaled_back,
    query_sum,
    key_sum,
    value_sum,
):
    devices, rows, _ = query.shape
    width = size * devices
    first_length = lengths[0]
    factor = HEAD_DIM ** (-0.5)
    key_sum[...] = jnp.zeros_like(key_sum)
    value_sum[...] = jnp.zeros_like(value_sum)

    def for_queries(index, carry):
        places = pair_block(at_col, index, size)[:, :1]
        held_now = []
        for head in range(held):
            pushed = pair_block(attended_back, index, size, head)
            row_dot = jnp.sum(
                pushed.astype(WIDE) * pair_block(attended, index, size, head).astype(WIDE),
                axis=1,
                keepdims=True,
            )
            logs = pair_block(log_total, index, size, head)[:, :1]
            held_now.append((pair_block(query, index, size, head), pushed, row_dot, logs))

        def for_keys(other, sums):
            seen = span_mask(places, at_row[other], first_length)
            here = pl.ds(pl.multiple_of(other * width, width), width)
            out_sums = []
            for head, (block, pushed, row_dot, logs) in enumerate(held_now):
                key_block = pair_block(keyed, other, size, head)
                raw = jnp.where(seen, mm_nt(block, key_block) * factor, NEG)
                probs = jnp.exp(raw - logs)
                prob_back = mm_nt(pushed, pair_block(value, other, size, head))
                score_back = (probs * (prob_back - row_dot)).astype(LOW)
                value_sum[head, here, :] += mm_tn(probs.astype(LOW), pushed)
                key_sum[head, here, :] += mm_tn(score_back, block)
                out_sums.append(sums[head] + mm(score_back, key_block))
            return tuple(out_sums)

        lowest = first_block(first_length, index, width)
        start = (jnp.zeros((width, HEAD_DIM), WIDE),) * held
        sums = lax.fori_loop(lowest, index + 1, for_keys, start)
        here = pl.ds(pl.multiple_of(index * width, width), width)
        for head in range(held):
            query_sum[head, here, :] = sums[head]
        return carry

    lax.fori_loop(0, rows // size, for_queries, 0)

    def finish(index, carry):
        wave, ripple = pair_block(cosine, index, size), pair_block(sine, index, size)
        scale = pair_block(scale_row, index, size)[:, :1]
        here = pl.ds(pl.multiple_of(index * width, width), width)
        for head in range(held):
            for place, source in ((0, query_sum), (held, key_sum)):
                block = source[head, here, :] * factor
                block = block * wave - pltpu.roll(block, HEAD_DIM // 2, 1) * ripple
                block = block.astype(LOW)
                put_block(projected_back, index, size, block, place + head)
                put_block(
                    scaled_back, index, size, (block.astype(WIDE) * scale).astype(LOW), place + head
                )
            block = value_sum[head, here, :].astype(LOW)
            put_block(projected_back, index, size, block, 2 * held + head)
            block = (block.astype(WIDE) * scale).astype(LOW)
            put_block(scaled_back, index, size, block, 2 * held + head)
        return carry

    lax.fori_loop(0, rows // size, finish, 0)


def attend(lengths, projected, cosine, sine, at_col, at_row, held, size):
    devices, rows, _ = projected.shape
    low = jax.ShapeDtypeStruct((devices, rows, held * HEAD_DIM), LOW)
    inside = pl.BlockSpec(memory_space=pltpu.VMEM)
    return pl.pallas_call(
        functools.partial(attend_kernel, size, held),
        in_specs=[pl.BlockSpec(memory_space=pltpu.SMEM)] + [inside] * 5,
        out_specs=[inside] * 5,
        out_shape=[low] * 4 + [jax.ShapeDtypeStruct(low.shape, WIDE)],
        cost_estimate=work(30),
        compiler_params=pltpu.CompilerParams(vmem_limit_bytes=56 * 2**20),
    )(lengths, projected, cosine, sine, at_col, at_row)


def attend_back(
    lengths, query, keyed, value, attended, pushed, log_total, cosine, sine, scale_row,
    at_col, at_row, held, size,
):
    devices, rows, _ = query.shape
    low = jax.ShapeDtypeStruct((devices, rows, 3 * held * HEAD_DIM), LOW)
    inside = pl.BlockSpec(memory_space=pltpu.VMEM)
    return pl.pallas_call(
        functools.partial(attend_back_kernel, size, held),
        in_specs=[pl.BlockSpec(memory_space=pltpu.SMEM)] + [inside] * 11,
        out_specs=[inside] * 2,
        out_shape=[low] * 2,
        cost_estimate=work(1),
        scratch_shapes=[pltpu.VMEM((held, devices * rows, HEAD_DIM), WIDE)] * 3,
        compiler_params=pltpu.CompilerParams(vmem_limit_bytes=56 * 2**20),
    )(
        lengths, query, keyed, value, attended, pushed, log_total, cosine, sine, scale_row,
        at_col, at_row,
    )


def work(micros):
    return pl.CostEstimate(
        flops=int(micros * 1e9), bytes_accessed=int(micros * 3e6), transcendentals=0
    )


def chunks_of(total):
    return [(start, min(256, total - start)) for start in range(0, total, 256)]


def ring_blocks(block, devices, first, last):
    ring = [(i, (i + 2) % devices) for i in range(devices)]
    blocks = [block]
    for _ in range(first, last):
        blocks.append(lax.ppermute(blocks[-1], "fsdp", ring))
    return blocks


def ring_place(blocks, devices):
    mine = lax.axis_index("fsdp")
    twin = [(i, i ^ 1) for i in range(devices)]
    whole = jnp.zeros((devices,) + blocks[0].shape, blocks[0].dtype)
    for step, block in enumerate(blocks):
        owner = lax.rem(mine + devices - 2 * step, devices)
        whole = lax.dynamic_update_index_in_dim(whole, block, owner, 0)
        other = lax.ppermute(block, "fsdp", twin)
        whole = lax.dynamic_update_index_in_dim(whole, other, owner ^ 1, 0)
    return whole


def remote(source, target, sent, arrived, where):
    return pltpu.make_async_remote_copy(
        src_ref=source,
        dst_ref=target,
        send_sem=sent,
        recv_sem=arrived,
        device_id=where,
        device_id_type=pl.DeviceIdType.MESH,
    )


def open_kernel(peers):
    barrier = pltpu.get_barrier_semaphore()
    for peer in peers:
        pl.semaphore_signal(
            barrier, inc=1, device_id=peer, device_id_type=pl.DeviceIdType.MESH
        )
    pl.semaphore_wait(barrier, len(peers))


def middle_block(experts, rows, cot, weights, weight_down, named, spread, act_out, grad_out, strengths):
    total = act_out.shape[1]
    lane = lax.broadcasted_iota(jnp.int32, (rows.shape[0], 128), 1)
    logits = mm_nt(rows, weights[2 * total :, :])
    sigma = jax.nn.sigmoid(logits)
    masked = jnp.where((lane >= 1) & (lane <= experts), logits, NEG)
    lifted = jnp.exp(masked - jnp.max(masked, axis=1, keepdims=True))
    normal = lifted / jnp.sum(lifted, axis=1, keepdims=True)
    strength = jnp.where(lane == 0, sigma, normal * named)
    high = strength.astype(LOW)
    rest = (strength - high.astype(WIDE)).astype(LOW)
    strengths[...] = jnp.zeros_like(strengths)
    for start, size in chunks_of(total):
        here = pl.ds(start, size)
        gate = mm_nt(rows, weights[start : start + size, :])
        up = mm_nt(rows, weights[total + start : total + start + size, :])
        pushed = mm_nt(cot, weight_down[start : start + size, :])
        wide = mm(high, spread[:, here]) + mm(rest, spread[:, here])
        curve = jax.nn.sigmoid(gate)
        silu = gate * curve
        act = silu * up
        act_out[:, here] = (wide * act).astype(LOW)
        strengths[...] += mm_nt((act * pushed).astype(LOW), spread[:, here])
        pushed = wide * pushed
        grad_out[:, here] = (pushed * up * (curve + silu * (1.0 - curve))).astype(LOW)
        grad_out[:, pl.ds(total + start, size)] = (pushed * silu).astype(LOW)
    backs = strengths[...]
    gates_back = jnp.where(lane >= 1, backs * named, 0.0)
    logit_grad = normal * (gates_back - jnp.sum(normal * gates_back, axis=1, keepdims=True))
    logit_grad = jnp.where(lane == 0, backs * sigma * (1.0 - sigma), logit_grad)
    grad_out[:, 2 * total :] = logit_grad.astype(LOW)


def middle_kernel(
    devices,
    experts,
    hidden,
    cot_all,
    weights_far,
    down_far,
    chosen,
    spread,
    hidden_all,
    act_all,
    grad_all,
    weights,
    weight_down,
    strengths,
    ring_sent,
    ring_got,
    twin_sent,
    twin_got,
    local_done,
):
    mine = lax.axis_index("fsdp")
    steps = devices // 2
    rows, width = hidden.shape
    total = act_all.shape[2]
    right = lax.rem(mine + 2, devices)
    left = lax.rem(mine + devices - 2, devices)
    twin = mine + 1 - 2 * lax.rem(mine, 2)
    open_kernel([{"fsdp": right}, {"fsdp": left}, {"fsdp": twin}])
    loads = [
        pltpu.make_async_copy(hidden, hidden_all.at[mine], local_done.at[0]),
        pltpu.make_async_copy(weights_far, weights, local_done.at[1]),
        pltpu.make_async_copy(down_far, weight_down, local_done.at[2]),
    ]
    for one in loads:
        one.start()
    loads[0].wait()

    def along(s, where, sent, got):
        block = hidden_all.at[lax.rem(mine + devices - 2 * s, devices)]
        return remote(block, block, sent.at[s], got.at[s], {"fsdp": where})

    def body(rows_in, cot_in, named, act_out, grad_out):
        middle_block(
            experts,
            rows_in[0],
            cot_in[0],
            weights,
            weight_down,
            named[0].astype(WIDE),
            spread,
            act_out.at[0],
            grad_out.at[0],
            strengths,
        )

    def step(s, carry):
        @pl.when(s > 0)
        def _():
            along(s - 1, right, ring_sent, ring_got).wait_recv()

        @pl.when(s < steps - 1)
        def _():
            along(s, right, ring_sent, ring_got).start()

        along(s, twin, twin_sent, twin_got).start()
        along(s, twin, twin_sent, twin_got).wait_recv()

        @pl.when(s == 0)
        def _():
            loads[1].wait()
            loads[2].wait()

        first = lax.rem(mine - lax.rem(mine, 2) + devices - 2 * s, devices)
        by_rows = lambda columns: pl.BlockSpec((1, rows, columns), lambda i: (first + i, 0, 0))
        pltpu.emit_pipeline(
            body,
            grid=(2,),
            in_specs=[by_rows(width), by_rows(width), by_rows(128)],
            out_specs=[by_rows(total), by_rows(2 * total + 128)],
        )(hidden_all, cot_all, chosen, act_all, grad_all)
        return carry

    lax.fori_loop(0, steps, step, 0)
    for s in range(steps):
        if s < steps - 1:
            along(s, right, ring_sent, ring_got).wait_send()
        along(s, twin, twin_sent, twin_got).wait_send()


def middle(hidden, cot_all, weights, weight_down, chosen, spread, experts):
    devices, rows, width = cot_all.shape
    total = weight_down.shape[0]
    dma = pltpu.SemaphoreType.DMA
    anywhere = pl.BlockSpec(memory_space=pl.ANY)
    inside = pl.BlockSpec(memory_space=pltpu.VMEM)
    low = lambda columns: jax.ShapeDtypeStruct((devices, rows, columns), LOW)
    return pl.pallas_call(
        functools.partial(middle_kernel, devices, experts),
        in_specs=[inside, anywhere, anywhere, anywhere, anywhere, inside],
        out_specs=[anywhere] * 3,
        out_shape=[low(width), low(total), low(2 * total + 128)],
        scratch_shapes=[
            pltpu.VMEM(weights.shape, LOW),
            pltpu.VMEM(weight_down.shape, LOW),
            pltpu.VMEM((rows, 128), WIDE),
            dma((devices // 2,)),
            dma((devices // 2,)),
            dma((devices // 2,)),
            dma((devices // 2,)),
            dma((3,)),
        ],
        cost_estimate=work(110),
        compiler_params=pltpu.CompilerParams(
            collective_id=1, has_side_effects=True, vmem_limit_bytes=60 * 2**20
        ),
    )(hidden, cot_all, weights, weight_down, chosen, spread)


def gather_kernel(
    devices,
    reps,
    token,
    strip,
    share,
    small,
    token_all,
    strip_all,
    share_all,
    small_all,
    ring_sent,
    ring_got,
    twin_sent,
    twin_got,
    deal_sent,
    deal_got,
    rep_sent,
    rep_got,
    share_sent,
    share_got,
    pass_sent,
    pass_got,
    local_done,
):
    mine = lax.axis_index("fsdp")
    copy = lax.axis_index("rep")
    steps = devices // 2
    right = lax.rem(mine + 2, devices)
    twin = mine + 1 - 2 * lax.rem(mine, 2)
    around = [{"fsdp": lax.rem(mine + k, devices)} for k in range(1, devices)]
    across = [{"rep": lax.rem(copy + k, reps)} for k in range(1, reps)]
    open_kernel(around + across)

    owners = [lax.rem(mine + devices - 2 * s, devices) for s in range(steps)]
    inputs = (token, share, small)
    whole = (token_all, share_all.at[:, copy], small_all)
    everything = []

    def begin(one):
        one.start()
        everything.append(one)
        return one

    locals_ = [
        pltpu.make_async_copy(token, token_all.at[mine], local_done.at[0]),
        pltpu.make_async_copy(share, share_all.at[mine, copy], local_done.at[1]),
        pltpu.make_async_copy(small, small_all.at[mine], local_done.at[2]),
        pltpu.make_async_copy(strip.at[mine], strip_all.at[mine, copy], local_done.at[3]),
    ]
    def ring_step(j, s):
        source = inputs[j] if s == 0 else whole[j].at[owners[s]]
        if s + 1 < steps:
            begin(
                remote(
                    source,
                    whole[j].at[owners[s]],
                    ring_sent.at[j, s],
                    ring_got.at[j, s],
                    {"fsdp": right},
                )
            )
        begin(
            remote(
                source,
                whole[j].at[owners[s]],
                twin_sent.at[j, s],
                twin_got.at[j, s],
                {"fsdp": twin},
            )
        )

    def ring_wait(j, s):
        remote(
            inputs[j],
            whole[j].at[owners[s + 1]],
            ring_sent.at[j, s],
            ring_got.at[j, s],
            {"fsdp": right},
        ).wait_recv()

    shared = {}

    def share_cross(s):
        source = share if s == 0 else share_all.at[owners[s], copy]
        for k in range(1, reps):
            shared[k, s] = begin(
                remote(
                    source,
                    share_all.at[owners[s], copy],
                    share_sent.at[k - 1, s],
                    share_got.at[k - 1, s],
                    {"rep": lax.rem(copy + k, reps)},
                )
            )

    ring_step(1, 0)
    ring_step(2, 0)
    ring_step(0, 0)
    deals = []
    for k in range(1, devices):
        peer = lax.rem(mine + k, devices)
        deals.append(
            begin(
                remote(
                    strip.at[peer],
                    strip_all.at[mine, copy],
                    deal_sent.at[k - 1],
                    deal_got.at[k - 1],
                    {"fsdp": peer},
                )
            )
        )
    share_cross(0)
    for one in locals_:
        one.start()
    for s in range(1, steps):
        for j in (1, 2):
            ring_wait(j, s - 1)
            ring_step(j, s)
        share_cross(s)
    if steps > 1:
        ring_wait(0, 0)
        ring_step(0, 1)
    locals_[3].wait()
    for one in deals:
        one.wait_recv()
    crossed = []
    for k in range(1, reps):
        crossed.append(
            begin(
                remote(
                    strip_all.at[:, copy],
                    strip_all.at[:, copy],
                    rep_sent.at[k - 1],
                    rep_got.at[k - 1],
                    {"rep": lax.rem(copy + k, reps)},
                )
            )
        )
    if steps > 2:
        ring_wait(0, 1)
        ring_step(0, 2)
    for s in range(steps):
        for k in range(1, reps):
            origin = lax.rem(copy + reps - k, reps)
            shared[k, s].wait_recv()
            begin(
                remote(
                    share_all.at[owners[s], origin],
                    share_all.at[owners[s], origin],
                    pass_sent.at[k - 1, s],
                    pass_got.at[k - 1, s],
                    {"fsdp": twin},
                )
            )
    for s in range(3, steps):
        ring_wait(0, s - 1)
        ring_step(0, s)
    for one in everything:
        one.wait_send()
    for j in range(3):
        for s in range(steps):
            remote(
                inputs[j],
                whole[j].at[owners[s]],
                twin_sent.at[j, s],
                twin_got.at[j, s],
                {"fsdp": twin},
            ).wait_recv()
    for one in crossed:
        one.wait_recv()
    for k in range(1, reps):
        for s in range(steps):
            remote(
                share,
                share_all.at[owners[s], copy],
                pass_sent.at[k - 1, s],
                pass_got.at[k - 1, s],
                {"fsdp": twin},
            ).wait_recv()
    for one in locals_[:3]:
        one.wait()


def gather_all(token, strip, share, small, reps):
    devices, piece, columns = strip.shape
    steps = devices // 2
    dma = pltpu.SemaphoreType.DMA
    anywhere = pl.BlockSpec(memory_space=pl.ANY)
    return pl.pallas_call(
        functools.partial(gather_kernel, devices, reps),
        in_specs=[pl.BlockSpec(memory_space=pltpu.VMEM)] * 4,
        out_specs=[anywhere] * 4,
        out_shape=[
            jax.ShapeDtypeStruct((devices,) + token.shape, LOW),
            jax.ShapeDtypeStruct((devices, reps, piece, columns), LOW),
            jax.ShapeDtypeStruct((devices, reps) + share.shape, LOW),
            jax.ShapeDtypeStruct((devices,) + small.shape, LOW),
        ],
        scratch_shapes=[
            dma((3, steps)),
            dma((3, steps)),
            dma((3, steps)),
            dma((3, steps)),
            dma((devices - 1,)),
            dma((devices - 1,)),
            dma((reps - 1,)),
            dma((reps - 1,)),
            dma((reps - 1, steps)),
            dma((reps - 1, steps)),
            dma((reps - 1, steps)),
            dma((reps - 1, steps)),
            dma((4,)),
        ],
        cost_estimate=work(100),
        compiler_params=pltpu.CompilerParams(collective_id=0, has_side_effects=True),
    )(token, strip, share, small)


def reduce_rep(values):
    return lax.psum(values, "rep")


def shards(
    tokens,
    lengths,
    dealing,
    routes,
    cotangent,
    first_gain,
    projection,
    projection_bias,
    output_weight,
    second_gain,
    router_weight,
    shared_gate,
    shared_in,
    shared_out,
    expert_in,
    expert_out,
):
    width = tokens.shape[1]
    rows = tokens.shape[0]
    group = dealing.shape[0]
    devices = group // rows
    part = width // devices
    held = part // HEAD_DIM
    experts, _, _, units = expert_in.shape
    hidden = -(-units // 16) * 16
    common = shared_out.shape[0]
    total = common + experts * hidden
    reps = lax.axis_size("rep")
    piece = part // reps
    mine = lax.axis_index("fsdp")
    copy = lax.axis_index("rep")
    scale = HEAD_DIM ** (-0.5)

    gain_one = first_gain.astype(WIDE)
    strip = lax.dynamic_slice_in_dim(projection, copy * piece, piece, 0).astype(WIDE)
    strip = (lax.dynamic_slice_in_dim(gain_one, copy * piece, piece, 0)[:, None] * strip).astype(LOW)
    strip = strip.reshape(piece, 3, devices, part).transpose(2, 0, 1, 3)
    strip = strip.reshape(devices, piece, 3 * part)
    share = lax.dynamic_slice_in_dim(output_weight, copy * piece, piece, 0)
    small = jnp.concatenate(
        [second_gain, shared_gate, projection_bias, router_weight.reshape(-1)]
    )
    length = small.shape[0]
    small = jnp.pad(small, (0, -length % 2048)).reshape(-1, 128)
    token_all, strip, share, small = gather_all(tokens, strip, share, small, reps)
    token_all = token_all.reshape(group, width)
    weight_mine = strip.reshape(width, 3 * part)
    weight_output = share.reshape(width, width)
    small = small.reshape(devices, -1)[:, :length]
    cot_in, _ = lax.optimization_barrier((cotangent, token_all))
    steps = devices // 2
    cot_blocks = ring_blocks(cot_in, devices, 0, 1)

    gain_two = small[:, :part].reshape(width).astype(WIDE)
    gate_weight = small[:, part : 2 * part].reshape(width, 1)
    bias = small[:, 2 * part : 5 * part].reshape(3, devices, part)
    bias_mine = lax.dynamic_slice_in_dim(bias, mine, 1, 1).reshape(3 * part).astype(WIDE)
    router = small[:, 5 * part :].reshape(width, experts)
    choice_weight = jnp.concatenate(
        [gate_weight, router, jnp.zeros((width, 127 - experts), LOW)], axis=1
    )
    scale_all = scale_of(token_all.astype(WIDE))
    projected = scale_all * mm(token_all, weight_mine) + bias_mine
    first_length = lengths[0, 0]
    second = (dealing >= first_length).astype(jnp.int32)
    cosine, sine = rope_tables(dealing - second * first_length)
    shape = (devices, rows, HEAD_DIM)
    cosine = jnp.concatenate([cosine, cosine], axis=1).reshape(shape)
    sine = jnp.concatenate([-sine, sine], axis=1).reshape(shape)
    size = 256 // devices
    at_col = jnp.broadcast_to(dealing.reshape(devices, rows, 1), shape)
    at_row = dealing.reshape(devices, rows // size, size).transpose(1, 0, 2)
    at_row = at_row.reshape(rows // size, 1, devices * size)
    scale_row = jnp.broadcast_to(scale_all.reshape(devices, rows, 1), shape)
    projected, first_step = lax.optimization_barrier((projected, cot_blocks[1]))
    cot_blocks = [cot_blocks[0]] + ring_blocks(first_step, devices, 1, steps // 2)
    query, keyed, value, attended_mine, log_total = attend(
        lengths[0], projected.reshape(devices, rows, 3 * part), cosine, sine, at_col, at_row,
        held, size,
    )
    attended = attended_mine.reshape(group, part)
    cot_blocks = cot_blocks[:-1] + ring_blocks(cot_blocks[-1], devices, steps // 2, steps - 1)
    cot_all = ring_place(cot_blocks, devices).reshape(group, width)
    full = -(-total // 128) * 128
    shared_in, shared_out, expert_in, expert_out, _ = lax.optimization_barrier(
        (shared_in, shared_out, expert_in, expert_out, attended_mine)
    )
    expert_rows = expert_in.transpose(0, 1, 3, 2)
    expert_down = expert_out
    if hidden > units:
        expert_rows = jnp.pad(expert_rows, ((0, 0), (0, 0), (0, hidden - units), (0, 0)))
        expert_down = jnp.pad(expert_down, ((0, 0), (0, hidden - units), (0, 0)))
    fill = jnp.zeros((full - total, width), LOW)
    weights = []
    for half in range(2):
        weights.append(shared_in[half].T)
        weights.append(expert_rows[:, half].reshape(experts * hidden, width))
        weights.append(fill)
    weights = jnp.concatenate(weights + [choice_weight.T], axis=0)
    weight_down = jnp.concatenate(
        [shared_out, expert_down.reshape(experts * hidden, width), fill], axis=0
    )

    attended = lax.all_to_all(attended, "fsdp", split_axis=0, concat_axis=1, tiled=True)

    residual = tokens.astype(WIDE) + mm(attended, weight_output)
    scale_two = scale_of(residual)
    unit = residual * scale_two
    hidden_two = (unit * gain_two).astype(LOW)
    lane = jnp.arange(128, dtype=jnp.int32)
    chosen = jnp.any(routes[:, :, None] + 1 == lane[None, None, :], axis=1).astype(LOW)
    owner = jnp.concatenate(
        [
            jnp.zeros((common,), jnp.int32),
            1 + jnp.repeat(jnp.arange(experts, dtype=jnp.int32), hidden),
            jnp.full((full - total,), 127, jnp.int32),
        ]
    )
    spread = (owner[None, :] == lane[:, None]).astype(LOW)
    hidden_all, act_low, grads = middle(
        hidden_two,
        cot_all.reshape(devices, rows, width),
        weights,
        weight_down,
        chosen.reshape(devices, rows, 128),
        spread,
        experts,
    )
    hidden_all = hidden_all.reshape(group, width)
    act_low = act_low.reshape(group, full)
    grads = grads.reshape(group, 2 * full + 128)

    down_grad = mm_tn(act_low, cot_all, LOW)
    grads, down_grad = lax.optimization_barrier((grads, down_grad))
    down_grad = reduce_rep(down_grad)
    hidden_back = mm(grads, weights, LOW)
    act_low, grads, hidden_back = lax.optimization_barrier((act_low, grads, hidden_back))
    hidden_back = lax.psum_scatter(hidden_back, "fsdp", scatter_dimension=0, tiled=True)
    hidden_back = hidden_back.astype(WIDE)
    in_grad = mm_tn(grads, hidden_all, LOW)
    choice_weight_grad = in_grad[2 * full :].T
    in_grad, down_grad = lax.optimization_barrier((in_grad, down_grad))
    in_grad = reduce_rep(in_grad)
    layered = mm(act_low, weight_down, LOW)

    gain_two_grad = jnp.sum(hidden_back * unit, axis=0)
    pushed = hidden_back * gain_two
    residual_grad = cotangent.astype(WIDE) + scale_two * (
        pushed - unit * jnp.mean(pushed * unit, axis=-1, keepdims=True)
    )
    output_low = residual_grad.astype(LOW)
    attended_back = mm_nt(output_low, weight_output, LOW)
    attended_back = lax.all_to_all(
        attended_back, "fsdp", split_axis=1, concat_axis=0, tiled=True
    ).reshape(devices, rows, part)
    attended_back, attended_held = lax.optimization_barrier((attended_back, attended))
    lane = jnp.arange(128, dtype=jnp.int32)
    extra = jnp.where(
        lane[None, :] == experts + 1, gain_two_grad[:, None].astype(LOW), choice_weight_grad
    )
    output_grad = jnp.concatenate([mm_tn(attended_held, output_low, LOW), extra], axis=1)
    output_grad = lax.psum_scatter(output_grad, "fsdp", scatter_dimension=0, tiled=True)

    parts = attend_back(
        lengths[0], query, keyed, value, attended_mine, attended_back, log_total, cosine, sine,
        scale_row, at_col, at_row, held, size,
    )
    projected_back = parts[0].reshape(group, 3 * part)
    scaled_back = parts[1].reshape(group, 3 * part)
    bias_grad = jnp.sum(projected_back.astype(WIDE), axis=0)
    weight_grad = mm_tn(token_all, scaled_back, LOW)
    bias_rows = jnp.broadcast_to(
        bias_grad.astype(LOW).reshape(1, 1, 3, part), (devices, 16, 3, part)
    )
    weight_grad = jnp.concatenate([weight_grad.reshape(devices, part, 3, part), bias_rows], axis=1)
    weight_grad = lax.all_to_all(
        weight_grad, "fsdp", split_axis=0, concat_axis=2, tiled=False
    ).reshape(part + 16, 3 * width)
    weight_grad, projected_back = lax.optimization_barrier((weight_grad, projected_back))
    token_back = mm_nt(projected_back, weight_mine, LOW)
    layered = lax.psum_scatter(layered, "fsdp", scatter_dimension=0, tiled=True)
    output_grad, weight_grad, in_grad, down_grad, layered = lax.optimization_barrier(
        (output_grad, weight_grad, in_grad, down_grad, layered)
    )
    weight_grad, output_grad = reduce_rep((weight_grad, output_grad))
    pushed = lax.psum_scatter(token_back, "fsdp", scatter_dimension=0, tiled=True).astype(WIDE)
    mixed = (residual + layered.astype(WIDE)).astype(LOW)
    bias_grad = weight_grad[part].astype(WIDE).reshape(devices, 3 * part)
    bias_grad = lax.dynamic_slice_in_dim(bias_grad, mine, 1, 0)[0]
    weight_grad = weight_grad[:part].astype(WIDE)
    small = output_grad[:, width:].astype(WIDE)
    output_grad = output_grad[:, :width].astype(WIDE)
    first_gain_grad = jnp.sum(weight_grad * projection.astype(WIDE), axis=1)
    projection_grad = weight_grad * gain_one[:, None]

    inputs = tokens.astype(WIDE)
    scale_one = scale_of(inputs)
    unit_one = inputs * scale_one
    tokens_grad = residual_grad + scale_one * (
        pushed - unit_one * jnp.mean(pushed * unit_one, axis=-1, keepdims=True)
    )

    in_grad = in_grad[: 2 * full].reshape(2, full, width)
    shared_in_grad = in_grad[:, :common].astype(WIDE).transpose(0, 2, 1)
    expert_in_grad = in_grad[:, common:total].reshape(2, experts, hidden, width)
    expert_in_grad = expert_in_grad[:, :, :units].astype(WIDE).transpose(1, 0, 3, 2)
    down_grad = down_grad.astype(WIDE)
    return (
        mixed,
        tokens_grad,
        first_gain_grad,
        projection_grad,
        bias_grad,
        output_grad,
        small[:, experts + 1],
        small[:, 1 : experts + 1],
        small[:, 0],
        shared_in_grad,
        down_grad[:common],
        expert_in_grad,
        down_grad[common:total].reshape(experts, hidden, width)[:, :units],
    )


def solution(mesh):
    in_specs = (
        P(("rep", "fsdp"), None),
        P("rep", None),
        P("rep"),
        P("rep", None),
        P(("rep", "fsdp"), None),
        P("fsdp"),
        P("fsdp", None),
        P("fsdp"),
        P("fsdp", None),
        P("fsdp"),
        P("fsdp", None),
        P("fsdp"),
        P(None, None, "fsdp"),
        P("fsdp", None),
        P(None, None, None, "fsdp"),
        P(None, "fsdp", None),
    )
    out_specs = (
        P(("rep", "fsdp"), None),
        P(("rep", "fsdp"), None),
        P("fsdp"),
        P("fsdp", None),
        P("fsdp"),
        P("fsdp", None),
        P("fsdp"),
        P("fsdp", None),
        P("fsdp"),
        P(None, None, "fsdp"),
        P("fsdp", None),
        P(None, None, None, "fsdp"),
        P(None, "fsdp", None),
    )
    return jax.shard_map(shards, mesh=mesh, in_specs=in_specs, out_specs=out_specs, check_vma=False)
```

```python
import functools

import jax
import jax.numpy as jnp
from jax import lax
from jax.experimental import pallas as pl
from jax.experimental.pallas import tpu as pltpu
from jax.sharding import PartitionSpec as P

HEAD_DIM = 128
EPS = 1e-06
THETA = 1000000.0
NEG = -1e30
LOW = jnp.bfloat16
WIDE = jnp.float32


def dot(left, right, dims, kind=WIDE):
    return lax.dot_general(left, right, ((dims[0], dims[1]), ((), ())), preferred_element_type=kind)


def mm(left, right, kind=WIDE):
    return dot(left, right, ((1,), (0,)), kind)


def mm_nt(left, right, kind=WIDE):
    return dot(left, right, ((1,), (1,)), kind)


def mm_tn(left, right, kind=WIDE):
    return dot(left, right, ((0,), (0,)), kind)


def scale_of(values):
    return lax.rsqrt(jnp.mean(values * values, axis=-1, keepdims=True) + EPS)


def rope_tables(position):
    half = HEAD_DIM // 2
    freq = THETA ** (-(jnp.arange(half, dtype=WIDE) * (2.0 / HEAD_DIM)))
    angle = position.astype(WIDE)[:, None] * freq[None, :]
    return (jnp.cos(angle), jnp.sin(angle))


def pair_block(ref, index, size, head=0):
    block = ref[
        :,
        pl.ds(pl.multiple_of(index * size, size), size),
        head * HEAD_DIM : (head + 1) * HEAD_DIM,
    ]
    return block.reshape(block.shape[0] * size, HEAD_DIM)


def put_block(ref, index, size, block, head=0):
    ref[
        :,
        pl.ds(pl.multiple_of(index * size, size), size),
        head * HEAD_DIM : (head + 1) * HEAD_DIM,
    ] = block.reshape(ref.shape[0], size, HEAD_DIM)


def first_block(first_length, index, width):
    return jnp.where(index * width >= first_length, first_length // width, 0)


def span_mask(at_col, at_row, first_length):
    lowest = jnp.where(at_col >= first_length, first_length, 0)
    return (at_row <= at_col) & (at_row >= lowest)


def attend_kernel(
    size,
    held,
    lengths,
    projected,
    cosine,
    sine,
    at_col,
    at_row,
    query,
    keyed,
    value,
    out,
    log_total,
):
    devices, rows, _ = projected.shape
    width = size * devices
    first_length = lengths[0]
    factor = HEAD_DIM ** (-0.5)

    def prepare(index, carry):
        wave, ripple = pair_block(cosine, index, size), pair_block(sine, index, size)
        for head in range(held):
            for place, target in ((0, query), (held, keyed)):
                block = pair_block(projected, index, size, place + head)
                block = block * wave + pltpu.roll(block, HEAD_DIM // 2, 1) * ripple
                put_block(target, index, size, block.astype(LOW), head)
            block = pair_block(projected, index, size, 2 * held + head)
            put_block(value, index, size, block.astype(LOW), head)
        return carry

    lax.fori_loop(0, rows // size, prepare, 0)

    def for_queries(index, carry):
        blocks = [pair_block(query, index, size, head) for head in range(held)]
        places = pair_block(at_col, index, size)[:, :1]

        def for_keys(other, states):
            seen = span_mask(places, at_row[other], first_length)
            out_states = []
            for head, (peak, total, summed) in enumerate(states):
                raw = mm_nt(blocks[head], pair_block(keyed, other, size, head)) * factor
                raw = jnp.where(seen, raw, NEG)
                higher = jnp.maximum(peak, jnp.max(raw, axis=1, keepdims=True))
                lifted = jnp.exp(raw - higher)
                fade = jnp.exp(peak - higher)
                total = total * fade + jnp.sum(lifted, axis=1, keepdims=True)
                summed = summed * fade + mm(
                    lifted.astype(LOW), pair_block(value, other, size, head)
                )
                out_states.append((higher, total, summed))
            return tuple(out_states)

        start = (
            jnp.full((width, 1), 2 * NEG, WIDE),
            jnp.zeros((width, 1), WIDE),
            jnp.zeros((width, HEAD_DIM), WIDE),
        )
        lowest = first_block(first_length, index, width)
        states = lax.fori_loop(lowest, index + 1, for_keys, (start,) * held)
        for head, (peak, total, summed) in enumerate(states):
            put_block(out, index, size, (summed / total).astype(LOW), head)
            logs = jnp.broadcast_to(peak + jnp.log(total), (width, HEAD_DIM))
            put_block(log_total, index, size, logs, head)
        return carry

    lax.fori_loop(0, rows // size, for_queries, 0)


def attend_back_kernel(
    size,
    held,
    lengths,
    query,
    keyed,
    value,
    attended,
    attended_back,
    log_total,
    cosine,
    sine,
    scale_row,
    at_col,
    at_row,
    projected_back,
    scaled_back,
    query_sum,
    key_sum,
    value_sum,
):
    devices, rows, _ = query.shape
    width = size * devices
    first_length = lengths[0]
    factor = HEAD_DIM ** (-0.5)
    key_sum[...] = jnp.zeros_like(key_sum)
    value_sum[...] = jnp.zeros_like(value_sum)

    def for_queries(index, carry):
        places = pair_block(at_col, index, size)[:, :1]
        held_now = []
        for head in range(held):
            pushed = pair_block(attended_back, index, size, head)
            row_dot = jnp.sum(
                pushed.astype(WIDE) * pair_block(attended, index, size, head).astype(WIDE),
                axis=1,
                keepdims=True,
            )
            logs = pair_block(log_total, index, size, head)[:, :1]
            held_now.append((pair_block(query, index, size, head), pushed, row_dot, logs))

        def for_keys(other, sums):
            seen = span_mask(places, at_row[other], first_length)
            here = pl.ds(pl.multiple_of(other * width, width), width)
            out_sums = []
            for head, (block, pushed, row_dot, logs) in enumerate(held_now):
                key_block = pair_block(keyed, other, size, head)
                raw = jnp.where(seen, mm_nt(block, key_block) * factor, NEG)
                probs = jnp.exp(raw - logs)
                prob_back = mm_nt(pushed, pair_block(value, other, size, head))
                score_back = (probs * (prob_back - row_dot)).astype(LOW)
                value_sum[head, here, :] += mm_tn(probs.astype(LOW), pushed)
                key_sum[head, here, :] += mm_tn(score_back, block)
                out_sums.append(sums[head] + mm(score_back, key_block))
            return tuple(out_sums)

        lowest = first_block(first_length, index, width)
        start = (jnp.zeros((width, HEAD_DIM), WIDE),) * held
        sums = lax.fori_loop(lowest, index + 1, for_keys, start)
        here = pl.ds(pl.multiple_of(index * width, width), width)
        for head in range(held):
            query_sum[head, here, :] = sums[head]
        return carry

    lax.fori_loop(0, rows // size, for_queries, 0)

    def finish(index, carry):
        wave, ripple = pair_block(cosine, index, size), pair_block(sine, index, size)
        scale = pair_block(scale_row, index, size)[:, :1]
        here = pl.ds(pl.multiple_of(index * width, width), width)
        for head in range(held):
            for place, source in ((0, query_sum), (held, key_sum)):
                block = source[head, here, :] * factor
                block = block * wave - pltpu.roll(block, HEAD_DIM // 2, 1) * ripple
                block = block.astype(LOW)
                put_block(projected_back, index, size, block, place + head)
                put_block(
                    scaled_back, index, size, (block.astype(WIDE) * scale).astype(LOW), place + head
                )
            block = value_sum[head, here, :].astype(LOW)
            put_block(projected_back, index, size, block, 2 * held + head)
            block = (block.astype(WIDE) * scale).astype(LOW)
            put_block(scaled_back, index, size, block, 2 * held + head)
        return carry

    lax.fori_loop(0, rows // size, finish, 0)


def attend(lengths, projected, cosine, sine, at_col, at_row, held, size):
    devices, rows, _ = projected.shape
    low = jax.ShapeDtypeStruct((devices, rows, held * HEAD_DIM), LOW)
    inside = pl.BlockSpec(memory_space=pltpu.VMEM)
    return pl.pallas_call(
        functools.partial(attend_kernel, size, held),
        in_specs=[pl.BlockSpec(memory_space=pltpu.SMEM)] + [inside] * 5,
        out_specs=[inside] * 5,
        out_shape=[low] * 4 + [jax.ShapeDtypeStruct(low.shape, WIDE)],
        cost_estimate=work(30),
        compiler_params=pltpu.CompilerParams(vmem_limit_bytes=56 * 2**20),
    )(lengths, projected, cosine, sine, at_col, at_row)


def attend_back(
    lengths, query, keyed, value, attended, pushed, log_total, cosine, sine, scale_row,
    at_col, at_row, held, size,
):
    devices, rows, _ = query.shape
    low = jax.ShapeDtypeStruct((devices, rows, 3 * held * HEAD_DIM), LOW)
    inside = pl.BlockSpec(memory_space=pltpu.VMEM)
    return pl.pallas_call(
        functools.partial(attend_back_kernel, size, held),
        in_specs=[pl.BlockSpec(memory_space=pltpu.SMEM)] + [inside] * 11,
        out_specs=[inside] * 2,
        out_shape=[low] * 2,
        cost_estimate=work(1),
        scratch_shapes=[pltpu.VMEM((held, devices * rows, HEAD_DIM), WIDE)] * 3,
        compiler_params=pltpu.CompilerParams(vmem_limit_bytes=56 * 2**20),
    )(
        lengths, query, keyed, value, attended, pushed, log_total, cosine, sine, scale_row,
        at_col, at_row,
    )


def work(micros):
    return pl.CostEstimate(
        flops=int(micros * 1e9), bytes_accessed=int(micros * 3e6), transcendentals=0
    )


def chunks_of(total):
    return [(start, min(256, total - start)) for start in range(0, total, 256)]


def ring_blocks(block, devices, first, last):
    ring = [(i, (i + 2) % devices) for i in range(devices)]
    blocks = [block]
    for _ in range(first, last):
        blocks.append(lax.ppermute(blocks[-1], "fsdp", ring))
    return blocks


def ring_place(blocks, devices):
    mine = lax.axis_index("fsdp")
    twin = [(i, i ^ 1) for i in range(devices)]
    whole = jnp.zeros((devices,) + blocks[0].shape, blocks[0].dtype)
    for step, block in enumerate(blocks):
        owner = lax.rem(mine + devices - 2 * step, devices)
        whole = lax.dynamic_update_index_in_dim(whole, block, owner, 0)
        other = lax.ppermute(block, "fsdp", twin)
        whole = lax.dynamic_update_index_in_dim(whole, other, owner ^ 1, 0)
    return whole


def remote(source, target, sent, arrived, where):
    return pltpu.make_async_remote_copy(
        src_ref=source,
        dst_ref=target,
        send_sem=sent,
        recv_sem=arrived,
        device_id=where,
        device_id_type=pl.DeviceIdType.MESH,
    )


def open_kernel(peers):
    barrier = pltpu.get_barrier_semaphore()
    for peer in peers:
        pl.semaphore_signal(
            barrier, inc=1, device_id=peer, device_id_type=pl.DeviceIdType.MESH
        )
    pl.semaphore_wait(barrier, len(peers))


def middle_block(experts, rows, cot, weights, weight_down, named, spread, act_out, grad_out, strengths):
    total = act_out.shape[1]
    lane = lax.broadcasted_iota(jnp.int32, (rows.shape[0], 128), 1)
    logits = mm_nt(rows, weights[2 * total :, :])
    sigma = jax.nn.sigmoid(logits)
    masked = jnp.where((lane >= 1) & (lane <= experts), logits, NEG)
    lifted = jnp.exp(masked - jnp.max(masked, axis=1, keepdims=True))
    normal = lifted / jnp.sum(lifted, axis=1, keepdims=True)
    strength = jnp.where(lane == 0, sigma, normal * named)
    high = strength.astype(LOW)
    rest = (strength - high.astype(WIDE)).astype(LOW)
    strengths[...] = jnp.zeros_like(strengths)
    for start, size in chunks_of(total):
        here = pl.ds(start, size)
        gate = mm_nt(rows, weights[start : start + size, :])
        up = mm_nt(rows, weights[total + start : total + start + size, :])
        pushed = mm_nt(cot, weight_down[start : start + size, :])
        wide = mm(high, spread[:, here]) + mm(rest, spread[:, here])
        curve = jax.nn.sigmoid(gate)
        silu = gate * curve
        act = silu * up
        act_out[:, here] = (wide * act).astype(LOW)
        strengths[...] += mm_nt((act * pushed).astype(LOW), spread[:, here])
        pushed = wide * pushed
        grad_out[:, here] = (pushed * up * (curve + silu * (1.0 - curve))).astype(LOW)
        grad_out[:, pl.ds(total + start, size)] = (pushed * silu).astype(LOW)
    backs = strengths[...]
    gates_back = jnp.where(lane >= 1, backs * named, 0.0)
    logit_grad = normal * (gates_back - jnp.sum(normal * gates_back, axis=1, keepdims=True))
    logit_grad = jnp.where(lane == 0, backs * sigma * (1.0 - sigma), logit_grad)
    grad_out[:, 2 * total :] = logit_grad.astype(LOW)


def middle_kernel(
    devices,
    experts,
    hidden,
    cot_all,
    weights_far,
    down_far,
    chosen,
    spread,
    hidden_all,
    act_all,
    grad_all,
    weights,
    weight_down,
    strengths,
    ring_sent,
    ring_got,
    twin_sent,
    twin_got,
    local_done,
):
    mine = lax.axis_index("fsdp")
    steps = devices // 2
    rows, width = hidden.shape
    total = act_all.shape[2]
    right = lax.rem(mine + 2, devices)
    left = lax.rem(mine + devices - 2, devices)
    twin = mine + 1 - 2 * lax.rem(mine, 2)
    open_kernel([{"fsdp": right}, {"fsdp": left}, {"fsdp": twin}])
    loads = [
        pltpu.make_async_copy(hidden, hidden_all.at[mine], local_done.at[0]),
        pltpu.make_async_copy(weights_far, weights, local_done.at[1]),
        pltpu.make_async_copy(down_far, weight_down, local_done.at[2]),
    ]
    for one in loads:
        one.start()
    loads[0].wait()

    def along(s, where, sent, got):
        block = hidden_all.at[lax.rem(mine + devices - 2 * s, devices)]
        return remote(block, block, sent.at[s], got.at[s], {"fsdp": where})

    def body(rows_in, cot_in, named, act_out, grad_out):
        middle_block(
            experts,
            rows_in[0],
            cot_in[0],
            weights,
            weight_down,
            named[0].astype(WIDE),
            spread,
            act_out.at[0],
            grad_out.at[0],
            strengths,
        )

    def step(s, carry):
        @pl.when(s > 0)
        def _():
            along(s - 1, right, ring_sent, ring_got).wait_recv()

        @pl.when(s < steps - 1)
        def _():
            along(s, right, ring_sent, ring_got).start()

        along(s, twin, twin_sent, twin_got).start()
        along(s, twin, twin_sent, twin_got).wait_recv()

        @pl.when(s == 0)
        def _():
            loads[1].wait()
            loads[2].wait()

        first = lax.rem(mine - lax.rem(mine, 2) + devices - 2 * s, devices)
        by_rows = lambda columns: pl.BlockSpec((1, rows, columns), lambda i: (first + i, 0, 0))
        pltpu.emit_pipeline(
            body,
            grid=(2,),
            in_specs=[by_rows(width), by_rows(width), by_rows(128)],
            out_specs=[by_rows(total), by_rows(2 * total + 128)],
        )(hidden_all, cot_all, chosen, act_all, grad_all)
        return carry

    lax.fori_loop(0, steps, step, 0)
    for s in range(steps):
        if s < steps - 1:
            along(s, right, ring_sent, ring_got).wait_send()
        along(s, twin, twin_sent, twin_got).wait_send()


def middle(hidden, cot_all, weights, weight_down, chosen, spread, experts):
    devices, rows, width = cot_all.shape
    total = weight_down.shape[0]
    dma = pltpu.SemaphoreType.DMA
    anywhere = pl.BlockSpec(memory_space=pl.ANY)
    inside = pl.BlockSpec(memory_space=pltpu.VMEM)
    low = lambda columns: jax.ShapeDtypeStruct((devices, rows, columns), LOW)
    return pl.pallas_call(
        functools.partial(middle_kernel, devices, experts),
        in_specs=[inside, anywhere, anywhere, anywhere, anywhere, inside],
        out_specs=[anywhere] * 3,
        out_shape=[low(width), low(total), low(2 * total + 128)],
        scratch_shapes=[
            pltpu.VMEM(weights.shape, LOW),
            pltpu.VMEM(weight_down.shape, LOW),
            pltpu.VMEM((rows, 128), WIDE),
            dma((devices // 2,)),
            dma((devices // 2,)),
            dma((devices // 2,)),
            dma((devices // 2,)),
            dma((3,)),
        ],
        cost_estimate=work(110),
        compiler_params=pltpu.CompilerParams(
            collective_id=1, has_side_effects=True, vmem_limit_bytes=60 * 2**20
        ),
    )(hidden, cot_all, weights, weight_down, chosen, spread)


def gather_kernel(
    devices,
    reps,
    token,
    strip,
    share,
    small,
    token_all,
    strip_all,
    share_all,
    small_all,
    ring_sent,
    ring_got,
    twin_sent,
    twin_got,
    deal_sent,
    deal_got,
    rep_sent,
    rep_got,
    share_sent,
    share_got,
    pass_sent,
    pass_got,
    local_done,
):
    mine = lax.axis_index("fsdp")
    copy = lax.axis_index("rep")
    steps = devices // 2
    right = lax.rem(mine + 2, devices)
    twin = mine + 1 - 2 * lax.rem(mine, 2)
    around = [{"fsdp": lax.rem(mine + k, devices)} for k in range(1, devices)]
    across = [{"rep": lax.rem(copy + k, reps)} for k in range(1, reps)]
    open_kernel(around + across)

    owners = [lax.rem(mine + devices - 2 * s, devices) for s in range(steps)]
    inputs = (token, share, small)
    whole = (token_all, share_all.at[:, copy], small_all)
    everything = []

    def begin(one):
        one.start()
        everything.append(one)
        return one

    locals_ = [
        pltpu.make_async_copy(token, token_all.at[mine], local_done.at[0]),
        pltpu.make_async_copy(share, share_all.at[mine, copy], local_done.at[1]),
        pltpu.make_async_copy(small, small_all.at[mine], local_done.at[2]),
        pltpu.make_async_copy(strip.at[mine], strip_all.at[mine, copy], local_done.at[3]),
    ]
    def ring_step(j, s):
        source = inputs[j] if s == 0 else whole[j].at[owners[s]]
        if s + 1 < steps:
            begin(
                remote(
                    source,
                    whole[j].at[owners[s]],
                    ring_sent.at[j, s],
                    ring_got.at[j, s],
                    {"fsdp": right},
                )
            )
        begin(
            remote(
                source,
                whole[j].at[owners[s]],
                twin_sent.at[j, s],
                twin_got.at[j, s],
                {"fsdp": twin},
            )
        )

    def ring_wait(j, s):
        remote(
            inputs[j],
            whole[j].at[owners[s + 1]],
            ring_sent.at[j, s],
            ring_got.at[j, s],
            {"fsdp": right},
        ).wait_recv()

    shared = {}

    def share_cross(s):
        source = share if s == 0 else share_all.at[owners[s], copy]
        for k in range(1, reps):
            shared[k, s] = begin(
                remote(
                    source,
                    share_all.at[owners[s], copy],
                    share_sent.at[k - 1, s],
                    share_got.at[k - 1, s],
                    {"rep": lax.rem(copy + k, reps)},
                )
            )

    ring_step(1, 0)
    ring_step(2, 0)
    ring_step(0, 0)
    deals = []
    for k in range(1, devices):
        peer = lax.rem(mine + k, devices)
        deals.append(
            begin(
                remote(
                    strip.at[peer],
                    strip_all.at[mine, copy],
                    deal_sent.at[k - 1],
                    deal_got.at[k - 1],
                    {"fsdp": peer},
                )
            )
        )
    share_cross(0)
    for one in locals_:
        one.start()
    for s in range(1, steps):
        for j in (1, 2):
            ring_wait(j, s - 1)
            ring_step(j, s)
        share_cross(s)
    if steps > 1:
        ring_wait(0, 0)
        ring_step(0, 1)
    locals_[3].wait()
    for one in deals:
        one.wait_recv()
    crossed = []
    for k in range(1, reps):
        crossed.append(
            begin(
                remote(
                    strip_all.at[:, copy],
                    strip_all.at[:, copy],
                    rep_sent.at[k - 1],
                    rep_got.at[k - 1],
                    {"rep": lax.rem(copy + k, reps)},
                )
            )
        )
    if steps > 2:
        ring_wait(0, 1)
        ring_step(0, 2)
    for s in range(steps):
        for k in range(1, reps):
            origin = lax.rem(copy + reps - k, reps)
            shared[k, s].wait_recv()
            begin(
                remote(
                    share_all.at[owners[s], origin],
                    share_all.at[owners[s], origin],
                    pass_sent.at[k - 1, s],
                    pass_got.at[k - 1, s],
                    {"fsdp": twin},
                )
            )
    for s in range(3, steps):
        ring_wait(0, s - 1)
        ring_step(0, s)
    for one in everything:
        one.wait_send()
    for j in range(3):
        for s in range(steps):
            remote(
                inputs[j],
                whole[j].at[owners[s]],
                twin_sent.at[j, s],
                twin_got.at[j, s],
                {"fsdp": twin},
            ).wait_recv()
    for one in crossed:
        one.wait_recv()
    for k in range(1, reps):
        for s in range(steps):
            remote(
                share,
                share_all.at[owners[s], copy],
                pass_sent.at[k - 1, s],
                pass_got.at[k - 1, s],
                {"fsdp": twin},
            ).wait_recv()
    for one in locals_[:3]:
        one.wait()


def gather_all(token, strip, share, small, reps):
    devices, piece, columns = strip.shape
    steps = devices // 2
    dma = pltpu.SemaphoreType.DMA
    anywhere = pl.BlockSpec(memory_space=pl.ANY)
    return pl.pallas_call(
        functools.partial(gather_kernel, devices, reps),
        in_specs=[pl.BlockSpec(memory_space=pltpu.VMEM)] * 4,
        out_specs=[anywhere] * 4,
        out_shape=[
            jax.ShapeDtypeStruct((devices,) + token.shape, LOW),
            jax.ShapeDtypeStruct((devices, reps, piece, columns), LOW),
            jax.ShapeDtypeStruct((devices, reps) + share.shape, LOW),
            jax.ShapeDtypeStruct((devices,) + small.shape, LOW),
        ],
        scratch_shapes=[
            dma((3, steps)),
            dma((3, steps)),
            dma((3, steps)),
            dma((3, steps)),
            dma((devices - 1,)),
            dma((devices - 1,)),
            dma((reps - 1,)),
            dma((reps - 1,)),
            dma((reps - 1, steps)),
            dma((reps - 1, steps)),
            dma((reps - 1, steps)),
            dma((reps - 1, steps)),
            dma((4,)),
        ],
        cost_estimate=work(100),
        compiler_params=pltpu.CompilerParams(collective_id=0, has_side_effects=True),
    )(token, strip, share, small)


def reduce_rep(values):
    return lax.psum(values, "rep")


def shards(
    tokens,
    lengths,
    dealing,
    routes,
    cotangent,
    first_gain,
    projection,
    projection_bias,
    output_weight,
    second_gain,
    router_weight,
    shared_gate,
    shared_in,
    shared_out,
    expert_in,
    expert_out,
):
    width = tokens.shape[1]
    rows = tokens.shape[0]
    group = dealing.shape[0]
    devices = group // rows
    part = width // devices
    held = part // HEAD_DIM
    experts, _, _, units = expert_in.shape
    hidden = -(-units // 16) * 16
    common = shared_out.shape[0]
    total = common + experts * hidden
    reps = lax.axis_size("rep")
    piece = part // reps
    mine = lax.axis_index("fsdp")
    copy = lax.axis_index("rep")
    scale = HEAD_DIM ** (-0.5)

    gain_one = first_gain.astype(WIDE)
    strip = lax.dynamic_slice_in_dim(projection, copy * piece, piece, 0).astype(WIDE)
    strip = (lax.dynamic_slice_in_dim(gain_one, copy * piece, piece, 0)[:, None] * strip).astype(LOW)
    strip = strip.reshape(piece, 3, devices, part).transpose(2, 0, 1, 3)
    strip = strip.reshape(devices, piece, 3 * part)
    share = lax.dynamic_slice_in_dim(output_weight, copy * piece, piece, 0)
    small = jnp.concatenate(
        [second_gain, shared_gate, projection_bias, router_weight.reshape(-1)]
    )
    length = small.shape[0]
    small = jnp.pad(small, (0, -length % 2048)).reshape(-1, 128)
    token_all, strip, share, small = gather_all(tokens, strip, share, small, reps)
    token_all = token_all.reshape(group, width)
    weight_mine = strip.reshape(width, 3 * part)
    weight_output = share.reshape(width, width)
    small = small.reshape(devices, -1)[:, :length]
    cot_in, _ = lax.optimization_barrier((cotangent, token_all))
    steps = devices // 2
    cot_blocks = ring_blocks(cot_in, devices, 0, 1)

    gain_two = small[:, :part].reshape(width).astype(WIDE)
    gate_weight = small[:, part : 2 * part].reshape(width, 1)
    bias = small[:, 2 * part : 5 * part].reshape(3, devices, part)
    bias_mine = lax.dynamic_slice_in_dim(bias, mine, 1, 1).reshape(3 * part).astype(WIDE)
    router = small[:, 5 * part :].reshape(width, experts)
    choice_weight = jnp.concatenate(
        [gate_weight, router, jnp.zeros((width, 127 - experts), LOW)], axis=1
    )
    scale_all = scale_of(token_all.astype(WIDE))
    projected = scale_all * mm(token_all, weight_mine) + bias_mine
    first_length = lengths[0, 0]
    second = (dealing >= first_length).astype(jnp.int32)
    cosine, sine = rope_tables(dealing - second * first_length)
    shape = (devices, rows, HEAD_DIM)
    cosine = jnp.concatenate([cosine, cosine], axis=1).reshape(shape)
    sine = jnp.concatenate([-sine, sine], axis=1).reshape(shape)
    size = 256 // devices
    at_col = jnp.broadcast_to(dealing.reshape(devices, rows, 1), shape)
    at_row = dealing.reshape(devices, rows // size, size).transpose(1, 0, 2)
    at_row = at_row.reshape(rows // size, 1, devices * size)
    scale_row = jnp.broadcast_to(scale_all.reshape(devices, rows, 1), shape)
    projected, first_step = lax.optimization_barrier((projected, cot_blocks[1]))
    cot_blocks = [cot_blocks[0]] + ring_blocks(first_step, devices, 1, steps // 2)
    query, keyed, value, attended_mine, log_total = attend(
        lengths[0], projected.reshape(devices, rows, 3 * part), cosine, sine, at_col, at_row,
        held, size,
    )
    attended = attended_mine.reshape(group, part)
    cot_blocks = cot_blocks[:-1] + ring_blocks(cot_blocks[-1], devices, steps // 2, steps - 1)
    cot_all = ring_place(cot_blocks, devices).reshape(group, width)
    full = -(-total // 128) * 128
    shared_in, shared_out, expert_in, expert_out, _ = lax.optimization_barrier(
        (shared_in, shared_out, expert_in, expert_out, attended_mine)
    )
    expert_rows = expert_in.transpose(0, 1, 3, 2)
    expert_down = expert_out
    if hidden > units:
        expert_rows = jnp.pad(expert_rows, ((0, 0), (0, 0), (0, hidden - units), (0, 0)))
        expert_down = jnp.pad(expert_down, ((0, 0), (0, hidden - units), (0, 0)))
    fill = jnp.zeros((full - total, width), LOW)
    weights = []
    for half in range(2):
        weights.append(shared_in[half].T)
        weights.append(expert_rows[:, half].reshape(experts * hidden, width))
        weights.append(fill)
    weights = jnp.concatenate(weights + [choice_weight.T], axis=0)
    weight_down = jnp.concatenate(
        [shared_out, expert_down.reshape(experts * hidden, width), fill], axis=0
    )

    attended = lax.all_to_all(attended, "fsdp", split_axis=0, concat_axis=1, tiled=True)

    residual = tokens.astype(WIDE) + mm(attended, weight_output)
    scale_two = scale_of(residual)
    unit = residual * scale_two
    hidden_two = (unit * gain_two).astype(LOW)
    lane = jnp.arange(128, dtype=jnp.int32)
    chosen = jnp.any(routes[:, :, None] + 1 == lane[None, None, :], axis=1).astype(LOW)
    owner = jnp.concatenate(
        [
            jnp.zeros((common,), jnp.int32),
            1 + jnp.repeat(jnp.arange(experts, dtype=jnp.int32), hidden),
            jnp.full((full - total,), 127, jnp.int32),
        ]
    )
    spread = (owner[None, :] == lane[:, None]).astype(LOW)
    hidden_all, act_low, grads = middle(
        hidden_two,
        cot_all.reshape(devices, rows, width),
        weights,
        weight_down,
        chosen.reshape(devices, rows, 128),
        spread,
        experts,
    )
    hidden_all = hidden_all.reshape(group, width)
    act_low = act_low.reshape(group, full)
    grads = grads.reshape(group, 2 * full + 128)

    down_grad = mm_tn(act_low, cot_all, LOW)
    grads, down_grad = lax.optimization_barrier((grads, down_grad))
    down_grad = reduce_rep(down_grad)
    hidden_back = mm(grads, weights, LOW)
    act_low, grads, hidden_back = lax.optimization_barrier((act_low, grads, hidden_back))
    hidden_back = lax.psum_scatter(hidden_back, "fsdp", scatter_dimension=0, tiled=True)
    hidden_back = hidden_back.astype(WIDE)
    in_grad = mm_tn(grads, hidden_all, LOW)
    choice_weight_grad = in_grad[2 * full :].T
    in_grad = jnp.concatenate([in_grad[:total], in_grad[full : full + total]], axis=0)
    in_grad, down_grad = lax.optimization_barrier((in_grad, down_grad))
    in_grad = reduce_rep(in_grad)
    layered = mm(act_low, weight_down, LOW)

    gain_two_grad = jnp.sum(hidden_back * unit, axis=0)
    pushed = hidden_back * gain_two
    residual_grad = cotangent.astype(WIDE) + scale_two * (
        pushed - unit * jnp.mean(pushed * unit, axis=-1, keepdims=True)
    )
    output_low = residual_grad.astype(LOW)
    attended_back = mm_nt(output_low, weight_output, LOW)
    attended_back = lax.all_to_all(
        attended_back, "fsdp", split_axis=1, concat_axis=0, tiled=True
    ).reshape(devices, rows, part)
    attended_back, attended_held = lax.optimization_barrier((attended_back, attended))
    lane = jnp.arange(128, dtype=jnp.int32)
    extra = jnp.where(
        lane[None, :] == experts + 1, gain_two_grad[:, None].astype(LOW), choice_weight_grad
    )
    output_grad = jnp.concatenate([mm_tn(attended_held, output_low, LOW), extra], axis=1)
    output_grad = lax.psum_scatter(output_grad, "fsdp", scatter_dimension=0, tiled=True)

    parts = attend_back(
        lengths[0], query, keyed, value, attended_mine, attended_back, log_total, cosine, sine,
        scale_row, at_col, at_row, held, size,
    )
    projected_back = parts[0].reshape(group, 3 * part)
    scaled_back = parts[1].reshape(group, 3 * part)
    bias_grad = jnp.sum(projected_back.astype(WIDE), axis=0)
    weight_grad = mm_tn(token_all, scaled_back, LOW)
    bias_rows = jnp.broadcast_to(
        bias_grad.astype(LOW).reshape(1, 1, 3, part), (devices, 16, 3, part)
    )
    weight_grad = jnp.concatenate([weight_grad.reshape(devices, part, 3, part), bias_rows], axis=1)
    weight_grad = lax.all_to_all(
        weight_grad, "fsdp", split_axis=0, concat_axis=2, tiled=False
    ).reshape(part + 16, 3 * width)
    weight_grad, projected_back = lax.optimization_barrier((weight_grad, projected_back))
    token_back = mm_nt(projected_back, weight_mine, LOW)
    layered = lax.psum_scatter(layered, "fsdp", scatter_dimension=0, tiled=True)
    output_grad, weight_grad, in_grad, down_grad, layered = lax.optimization_barrier(
        (output_grad, weight_grad, in_grad, down_grad, layered)
    )
    weight_grad, output_grad = reduce_rep((weight_grad, output_grad))
    pushed = lax.psum_scatter(token_back, "fsdp", scatter_dimension=0, tiled=True).astype(WIDE)
    mixed = (residual + layered.astype(WIDE)).astype(LOW)
    bias_grad = weight_grad[part].astype(WIDE).reshape(devices, 3 * part)
    bias_grad = lax.dynamic_slice_in_dim(bias_grad, mine, 1, 0)[0]
    weight_grad = weight_grad[:part].astype(WIDE)
    small = output_grad[:, width:].astype(WIDE)
    output_grad = output_grad[:, :width].astype(WIDE)
    first_gain_grad = jnp.sum(weight_grad * projection.astype(WIDE), axis=1)
    projection_grad = weight_grad * gain_one[:, None]

    inputs = tokens.astype(WIDE)
    scale_one = scale_of(inputs)
    unit_one = inputs * scale_one
    tokens_grad = residual_grad + scale_one * (
        pushed - unit_one * jnp.mean(pushed * unit_one, axis=-1, keepdims=True)
    )

    in_grad = in_grad.reshape(2, total, width)
    shared_in_grad = in_grad[:, :common].astype(WIDE).transpose(0, 2, 1)
    expert_in_grad = in_grad[:, common:].reshape(2, experts, hidden, width)
    expert_in_grad = expert_in_grad[:, :, :units].astype(WIDE).transpose(1, 0, 3, 2)
    down_grad = down_grad.astype(WIDE)
    return (
        mixed,
        tokens_grad,
        first_gain_grad,
        projection_grad,
        bias_grad,
        output_grad,
        small[:, experts + 1],
        small[:, 1 : experts + 1],
        small[:, 0],
        shared_in_grad,
        down_grad[:common],
        expert_in_grad,
        down_grad[common:total].reshape(experts, hidden, width)[:, :units],
    )


def solution(mesh):
    in_specs = (
        P(("rep", "fsdp"), None),
        P("rep", None),
        P("rep"),
        P("rep", None),
        P(("rep", "fsdp"), None),
        P("fsdp"),
        P("fsdp", None),
        P("fsdp"),
        P("fsdp", None),
        P("fsdp"),
        P("fsdp", None),
        P("fsdp"),
        P(None, None, "fsdp"),
        P("fsdp", None),
        P(None, None, None, "fsdp"),
        P(None, "fsdp", None),
    )
    out_specs = (
        P(("rep", "fsdp"), None),
        P(("rep", "fsdp"), None),
        P("fsdp"),
        P("fsdp", None),
        P("fsdp"),
        P("fsdp", None),
        P("fsdp"),
        P("fsdp", None),
        P("fsdp"),
        P(None, None, "fsdp"),
        P("fsdp", None),
        P(None, None, None, "fsdp"),
        P(None, "fsdp", None),
    )
    return jax.shard_map(shards, mesh=mesh, in_specs=in_specs, out_specs=out_specs, check_vma=False)
```

```python
import functools

import jax
import jax.numpy as jnp
from jax import lax
from jax.experimental import pallas as pl
from jax.experimental.pallas import tpu as pltpu
from jax.sharding import PartitionSpec as P

HEAD_DIM = 128
EPS = 1e-06
THETA = 1000000.0
NEG = -1e30
LOW = jnp.bfloat16
WIDE = jnp.float32


def dot(left, right, dims, kind=WIDE):
    return lax.dot_general(left, right, ((dims[0], dims[1]), ((), ())), preferred_element_type=kind)


def mm(left, right, kind=WIDE):
    return dot(left, right, ((1,), (0,)), kind)


def mm_nt(left, right, kind=WIDE):
    return dot(left, right, ((1,), (1,)), kind)


def mm_tn(left, right, kind=WIDE):
    return dot(left, right, ((0,), (0,)), kind)


def scale_of(values):
    return lax.rsqrt(jnp.mean(values * values, axis=-1, keepdims=True) + EPS)


def rope_tables(position):
    half = HEAD_DIM // 2
    freq = THETA ** (-(jnp.arange(half, dtype=WIDE) * (2.0 / HEAD_DIM)))
    angle = position.astype(WIDE)[:, None] * freq[None, :]
    return (jnp.cos(angle), jnp.sin(angle))


def pair_block(ref, index, size, head=0):
    block = ref[
        :,
        pl.ds(pl.multiple_of(index * size, size), size),
        head * HEAD_DIM : (head + 1) * HEAD_DIM,
    ]
    return block.reshape(block.shape[0] * size, HEAD_DIM)


def put_block(ref, index, size, block, head=0):
    ref[
        :,
        pl.ds(pl.multiple_of(index * size, size), size),
        head * HEAD_DIM : (head + 1) * HEAD_DIM,
    ] = block.reshape(ref.shape[0], size, HEAD_DIM)


def first_block(first_length, index, width):
    return jnp.where(index * width >= first_length, first_length // width, 0)


def span_mask(at_col, at_row, first_length):
    lowest = jnp.where(at_col >= first_length, first_length, 0)
    return (at_row <= at_col) & (at_row >= lowest)


def attend_kernel(
    size,
    held,
    lengths,
    projected,
    cosine,
    sine,
    at_col,
    at_row,
    query,
    keyed,
    value,
    out,
    log_total,
):
    devices, rows, _ = projected.shape
    width = size * devices
    first_length = lengths[0]
    factor = HEAD_DIM ** (-0.5)

    def prepare(index, carry):
        wave, ripple = pair_block(cosine, index, size), pair_block(sine, index, size)
        for head in range(held):
            for place, target in ((0, query), (held, keyed)):
                block = pair_block(projected, index, size, place + head)
                block = block * wave + pltpu.roll(block, HEAD_DIM // 2, 1) * ripple
                put_block(target, index, size, block.astype(LOW), head)
            block = pair_block(projected, index, size, 2 * held + head)
            put_block(value, index, size, block.astype(LOW), head)
        return carry

    lax.fori_loop(0, rows // size, prepare, 0)

    def for_queries(index, carry):
        blocks = [pair_block(query, index, size, head) for head in range(held)]
        places = pair_block(at_col, index, size)[:, :1]

        def for_keys(other, states):
            seen = span_mask(places, at_row[other], first_length)
            out_states = []
            for head, (peak, total, summed) in enumerate(states):
                raw = mm_nt(blocks[head], pair_block(keyed, other, size, head)) * factor
                raw = jnp.where(seen, raw, NEG)
                higher = jnp.maximum(peak, jnp.max(raw, axis=1, keepdims=True))
                lifted = jnp.exp(raw - higher)
                fade = jnp.exp(peak - higher)
                total = total * fade + jnp.sum(lifted, axis=1, keepdims=True)
                summed = summed * fade + mm(
                    lifted.astype(LOW), pair_block(value, other, size, head)
                )
                out_states.append((higher, total, summed))
            return tuple(out_states)

        start = (
            jnp.full((width, 1), 2 * NEG, WIDE),
            jnp.zeros((width, 1), WIDE),
            jnp.zeros((width, HEAD_DIM), WIDE),
        )
        lowest = first_block(first_length, index, width)
        states = lax.fori_loop(lowest, index + 1, for_keys, (start,) * held)
        for head, (peak, total, summed) in enumerate(states):
            put_block(out, index, size, (summed / total).astype(LOW), head)
            logs = jnp.broadcast_to(peak + jnp.log(total), (width, HEAD_DIM))
            put_block(log_total, index, size, logs, head)
        return carry

    lax.fori_loop(0, rows // size, for_queries, 0)


def attend_back_kernel(
    size,
    held,
    lengths,
    query,
    keyed,
    value,
    attended,
    attended_back,
    log_total,
    cosine,
    sine,
    scale_row,
    at_col,
    at_row,
    projected_back,
    scaled_back,
    query_sum,
    key_sum,
    value_sum,
):
    devices, rows, _ = query.shape
    width = size * devices
    first_length = lengths[0]
    factor = HEAD_DIM ** (-0.5)
    key_sum[...] = jnp.zeros_like(key_sum)
    value_sum[...] = jnp.zeros_like(value_sum)

    def for_queries(index, carry):
        places = pair_block(at_col, index, size)[:, :1]
        held_now = []
        for head in range(held):
            pushed = pair_block(attended_back, index, size, head)
            row_dot = jnp.sum(
                pushed.astype(WIDE) * pair_block(attended, index, size, head).astype(WIDE),
                axis=1,
                keepdims=True,
            )
            logs = pair_block(log_total, index, size, head)[:, :1]
            held_now.append((pair_block(query, index, size, head), pushed, row_dot, logs))

        def for_keys(other, sums):
            seen = span_mask(places, at_row[other], first_length)
            here = pl.ds(pl.multiple_of(other * width, width), width)
            out_sums = []
            for head, (block, pushed, row_dot, logs) in enumerate(held_now):
                key_block = pair_block(keyed, other, size, head)
                raw = jnp.where(seen, mm_nt(block, key_block) * factor, NEG)
                probs = jnp.exp(raw - logs)
                prob_back = mm_nt(pushed, pair_block(value, other, size, head))
                score_back = (probs * (prob_back - row_dot)).astype(LOW)
                value_sum[head, here, :] += mm_tn(probs.astype(LOW), pushed)
                key_sum[head, here, :] += mm_tn(score_back, block)
                out_sums.append(sums[head] + mm(score_back, key_block))
            return tuple(out_sums)

        lowest = first_block(first_length, index, width)
        start = (jnp.zeros((width, HEAD_DIM), WIDE),) * held
        sums = lax.fori_loop(lowest, index + 1, for_keys, start)
        here = pl.ds(pl.multiple_of(index * width, width), width)
        for head in range(held):
            query_sum[head, here, :] = sums[head]
        return carry

    lax.fori_loop(0, rows // size, for_queries, 0)

    def finish(index, carry):
        wave, ripple = pair_block(cosine, index, size), pair_block(sine, index, size)
        scale = pair_block(scale_row, index, size)[:, :1]
        here = pl.ds(pl.multiple_of(index * width, width), width)
        for head in range(held):
            for place, source in ((0, query_sum), (held, key_sum)):
                block = source[head, here, :] * factor
                block = block * wave - pltpu.roll(block, HEAD_DIM // 2, 1) * ripple
                block = block.astype(LOW)
                put_block(projected_back, index, size, block, place + head)
                put_block(
                    scaled_back, index, size, (block.astype(WIDE) * scale).astype(LOW), place + head
                )
            block = value_sum[head, here, :].astype(LOW)
            put_block(projected_back, index, size, block, 2 * held + head)
            block = (block.astype(WIDE) * scale).astype(LOW)
            put_block(scaled_back, index, size, block, 2 * held + head)
        return carry

    lax.fori_loop(0, rows // size, finish, 0)


def attend(lengths, projected, cosine, sine, at_col, at_row, held, size):
    devices, rows, _ = projected.shape
    low = jax.ShapeDtypeStruct((devices, rows, held * HEAD_DIM), LOW)
    inside = pl.BlockSpec(memory_space=pltpu.VMEM)
    return pl.pallas_call(
        functools.partial(attend_kernel, size, held),
        in_specs=[pl.BlockSpec(memory_space=pltpu.SMEM)] + [inside] * 5,
        out_specs=[inside] * 5,
        out_shape=[low] * 4 + [jax.ShapeDtypeStruct(low.shape, WIDE)],
        cost_estimate=work(30),
        compiler_params=pltpu.CompilerParams(vmem_limit_bytes=56 * 2**20),
    )(lengths, projected, cosine, sine, at_col, at_row)


def attend_back(
    lengths, query, keyed, value, attended, pushed, log_total, cosine, sine, scale_row,
    at_col, at_row, held, size,
):
    devices, rows, _ = query.shape
    low = jax.ShapeDtypeStruct((devices, rows, 3 * held * HEAD_DIM), LOW)
    inside = pl.BlockSpec(memory_space=pltpu.VMEM)
    return pl.pallas_call(
        functools.partial(attend_back_kernel, size, held),
        in_specs=[pl.BlockSpec(memory_space=pltpu.SMEM)] + [inside] * 11,
        out_specs=[inside] * 2,
        out_shape=[low] * 2,
        cost_estimate=work(1),
        scratch_shapes=[pltpu.VMEM((held, devices * rows, HEAD_DIM), WIDE)] * 3,
        compiler_params=pltpu.CompilerParams(vmem_limit_bytes=56 * 2**20),
    )(
        lengths, query, keyed, value, attended, pushed, log_total, cosine, sine, scale_row,
        at_col, at_row,
    )


def work(micros):
    return pl.CostEstimate(
        flops=int(micros * 1e9), bytes_accessed=int(micros * 3e6), transcendentals=0
    )


def chunks_of(total):
    return [(start, min(256, total - start)) for start in range(0, total, 256)]


def ring_blocks(block, devices, first, last):
    ring = [(i, (i + 2) % devices) for i in range(devices)]
    blocks = [block]
    for _ in range(first, last):
        blocks.append(lax.ppermute(blocks[-1], "fsdp", ring))
    return blocks


def ring_place(blocks, devices):
    mine = lax.axis_index("fsdp")
    twin = [(i, i ^ 1) for i in range(devices)]
    whole = jnp.zeros((devices,) + blocks[0].shape, blocks[0].dtype)
    for step, block in enumerate(blocks):
        owner = lax.rem(mine + devices - 2 * step, devices)
        whole = lax.dynamic_update_index_in_dim(whole, block, owner, 0)
        other = lax.ppermute(block, "fsdp", twin)
        whole = lax.dynamic_update_index_in_dim(whole, other, owner ^ 1, 0)
    return whole


def remote(source, target, sent, arrived, where):
    return pltpu.make_async_remote_copy(
        src_ref=source,
        dst_ref=target,
        send_sem=sent,
        recv_sem=arrived,
        device_id=where,
        device_id_type=pl.DeviceIdType.MESH,
    )


def open_kernel(peers):
    barrier = pltpu.get_barrier_semaphore()
    for peer in peers:
        pl.semaphore_signal(
            barrier, inc=1, device_id=peer, device_id_type=pl.DeviceIdType.MESH
        )
    pl.semaphore_wait(barrier, len(peers))


def middle_block(experts, rows, cot, weights, weight_down, named, spread, act_out, grad_out, strengths):
    total = act_out.shape[1]
    lane = lax.broadcasted_iota(jnp.int32, (rows.shape[0], 128), 1)
    logits = mm_nt(rows, weights[2 * total :, :])
    sigma = jax.nn.sigmoid(logits)
    masked = jnp.where((lane >= 1) & (lane <= experts), logits, NEG)
    lifted = jnp.exp(masked - jnp.max(masked, axis=1, keepdims=True))
    normal = lifted / jnp.sum(lifted, axis=1, keepdims=True)
    strength = jnp.where(lane == 0, sigma, normal * named)
    high = strength.astype(LOW)
    rest = (strength - high.astype(WIDE)).astype(LOW)
    strengths[...] = jnp.zeros_like(strengths)
    for start, size in chunks_of(total):
        here = pl.ds(start, size)
        gate = mm_nt(rows, weights[start : start + size, :])
        up = mm_nt(rows, weights[total + start : total + start + size, :])
        pushed = mm_nt(cot, weight_down[start : start + size, :])
        wide = mm(high, spread[:, here]) + mm(rest, spread[:, here])
        curve = jax.nn.sigmoid(gate)
        silu = gate * curve
        act = silu * up
        act_out[:, here] = (wide * act).astype(LOW)
        strengths[...] += mm_nt((act * pushed).astype(LOW), spread[:, here])
        pushed = wide * pushed
        grad_out[:, here] = (pushed * up * (curve + silu * (1.0 - curve))).astype(LOW)
        grad_out[:, pl.ds(total + start, size)] = (pushed * silu).astype(LOW)
    backs = strengths[...]
    gates_back = jnp.where(lane >= 1, backs * named, 0.0)
    logit_grad = normal * (gates_back - jnp.sum(normal * gates_back, axis=1, keepdims=True))
    logit_grad = jnp.where(lane == 0, backs * sigma * (1.0 - sigma), logit_grad)
    grad_out[:, 2 * total :] = logit_grad.astype(LOW)


def middle_kernel(
    devices,
    experts,
    hidden,
    cot_all,
    weights_far,
    down_far,
    chosen,
    spread,
    hidden_all,
    act_all,
    grad_all,
    weights,
    weight_down,
    strengths,
    ring_sent,
    ring_got,
    twin_sent,
    twin_got,
    local_done,
):
    mine = lax.axis_index("fsdp")
    steps = devices // 2
    rows, width = hidden.shape
    total = act_all.shape[2]
    right = lax.rem(mine + 2, devices)
    left = lax.rem(mine + devices - 2, devices)
    twin = mine + 1 - 2 * lax.rem(mine, 2)
    open_kernel([{"fsdp": right}, {"fsdp": left}, {"fsdp": twin}])
    loads = [
        pltpu.make_async_copy(hidden, hidden_all.at[mine], local_done.at[0]),
        pltpu.make_async_copy(weights_far, weights, local_done.at[1]),
        pltpu.make_async_copy(down_far, weight_down, local_done.at[2]),
    ]
    for one in loads:
        one.start()
    loads[0].wait()

    def along(s, where, sent, got):
        block = hidden_all.at[lax.rem(mine + devices - 2 * s, devices)]
        return remote(block, block, sent.at[s], got.at[s], {"fsdp": where})

    def body(rows_in, cot_in, named, act_out, grad_out):
        middle_block(
            experts,
            rows_in[0],
            cot_in[0],
            weights,
            weight_down,
            named[0].astype(WIDE),
            spread,
            act_out.at[0],
            grad_out.at[0],
            strengths,
        )

    def step(s, carry):
        @pl.when(s > 0)
        def _():
            along(s - 1, right, ring_sent, ring_got).wait_recv()

        @pl.when(s < steps - 1)
        def _():
            along(s, right, ring_sent, ring_got).start()

        along(s, twin, twin_sent, twin_got).start()
        along(s, twin, twin_sent, twin_got).wait_recv()

        @pl.when(s == 0)
        def _():
            loads[1].wait()
            loads[2].wait()

        first = lax.rem(mine - lax.rem(mine, 2) + devices - 2 * s, devices)
        by_rows = lambda columns: pl.BlockSpec((1, rows, columns), lambda i: (first + i, 0, 0))
        pltpu.emit_pipeline(
            body,
            grid=(2,),
            in_specs=[by_rows(width), by_rows(width), by_rows(128)],
            out_specs=[by_rows(total), by_rows(2 * total + 128)],
        )(hidden_all, cot_all, chosen, act_all, grad_all)
        return carry

    lax.fori_loop(0, steps, step, 0)
    for s in range(steps):
        if s < steps - 1:
            along(s, right, ring_sent, ring_got).wait_send()
        along(s, twin, twin_sent, twin_got).wait_send()


def middle(hidden, cot_all, weights, weight_down, chosen, spread, experts):
    devices, rows, width = cot_all.shape
    total = weight_down.shape[0]
    dma = pltpu.SemaphoreType.DMA
    anywhere = pl.BlockSpec(memory_space=pl.ANY)
    inside = pl.BlockSpec(memory_space=pltpu.VMEM)
    low = lambda columns: jax.ShapeDtypeStruct((devices, rows, columns), LOW)
    return pl.pallas_call(
        functools.partial(middle_kernel, devices, experts),
        in_specs=[inside, anywhere, anywhere, anywhere, anywhere, inside],
        out_specs=[anywhere] * 3,
        out_shape=[low(width), low(total), low(2 * total + 128)],
        scratch_shapes=[
            pltpu.VMEM(weights.shape, LOW),
            pltpu.VMEM(weight_down.shape, LOW),
            pltpu.VMEM((rows, 128), WIDE),
            dma((devices // 2,)),
            dma((devices // 2,)),
            dma((devices // 2,)),
            dma((devices // 2,)),
            dma((3,)),
        ],
        cost_estimate=work(110),
        compiler_params=pltpu.CompilerParams(
            collective_id=1, has_side_effects=True, vmem_limit_bytes=60 * 2**20
        ),
    )(hidden, cot_all, weights, weight_down, chosen, spread)


def gather_kernel(
    devices,
    reps,
    token,
    strip,
    share,
    small,
    token_all,
    strip_all,
    share_all,
    small_all,
    ring_sent,
    ring_got,
    twin_sent,
    twin_got,
    deal_sent,
    deal_got,
    rep_sent,
    rep_got,
    share_sent,
    share_got,
    pass_sent,
    pass_got,
    local_done,
):
    mine = lax.axis_index("fsdp")
    copy = lax.axis_index("rep")
    steps = devices // 2
    right = lax.rem(mine + 2, devices)
    twin = mine + 1 - 2 * lax.rem(mine, 2)
    around = [{"fsdp": lax.rem(mine + k, devices)} for k in range(1, devices)]
    across = [{"rep": lax.rem(copy + k, reps)} for k in range(1, reps)]
    open_kernel(around + across)

    owners = [lax.rem(mine + devices - 2 * s, devices) for s in range(steps)]
    half = token.shape[0] // 2
    inputs = (token.at[pl.ds(0, half)], share, small, token.at[pl.ds(half, half)])
    everything = []

    def spot(j, owner):
        if j == 1:
            return share_all.at[owner, copy]
        if j == 2:
            return small_all.at[owner]
        return token_all.at[owner, pl.ds(0 if j == 0 else half, half)]

    def begin(one):
        one.start()
        everything.append(one)
        return one

    locals_ = [
        pltpu.make_async_copy(token, token_all.at[mine], local_done.at[0]),
        pltpu.make_async_copy(share, share_all.at[mine, copy], local_done.at[1]),
        pltpu.make_async_copy(small, small_all.at[mine], local_done.at[2]),
        pltpu.make_async_copy(strip.at[mine], strip_all.at[mine, copy], local_done.at[3]),
    ]
    def ring_step(j, s):
        target = spot(j, owners[s])
        source = inputs[j] if s == 0 else target
        if s + 1 < steps:
            begin(
                remote(
                    source, target, ring_sent.at[j, s], ring_got.at[j, s], {"fsdp": right}
                )
            )
        begin(remote(source, target, twin_sent.at[j, s], twin_got.at[j, s], {"fsdp": twin}))

    def ring_pass(j, s):
        if 0 < s < steps:
            remote(
                inputs[j],
                spot(j, owners[s]),
                ring_sent.at[j, s - 1],
                ring_got.at[j, s - 1],
                {"fsdp": right},
            ).wait_recv()
            ring_step(j, s)

    shared = {}

    def share_cross(s):
        source = share if s == 0 else share_all.at[owners[s], copy]
        for k in range(1, reps):
            shared[k, s] = begin(
                remote(
                    source,
                    share_all.at[owners[s], copy],
                    share_sent.at[k - 1, s],
                    share_got.at[k - 1, s],
                    {"rep": lax.rem(copy + k, reps)},
                )
            )

    ring_step(1, 0)
    ring_step(2, 0)
    ring_step(0, 0)
    ring_step(3, 0)
    deals = []
    for k in range(1, devices):
        peer = lax.rem(mine + k, devices)
        deals.append(
            begin(
                remote(
                    strip.at[peer],
                    strip_all.at[mine, copy],
                    deal_sent.at[k - 1],
                    deal_got.at[k - 1],
                    {"fsdp": peer},
                )
            )
        )
    share_cross(0)
    for one in locals_:
        one.start()
    for s in range(1, steps):
        for j in (1, 2):
            ring_pass(j, s)
        share_cross(s)
        if s == 1:
            ring_pass(0, 1)
        if s == 2:
            ring_pass(3, 1)
    if steps == 2:
        ring_pass(3, 1)
    locals_[3].wait()
    for one in deals:
        one.wait_recv()
    crossed = []
    for k in range(1, reps):
        crossed.append(
            begin(
                remote(
                    strip_all.at[:, copy],
                    strip_all.at[:, copy],
                    rep_sent.at[k - 1],
                    rep_got.at[k - 1],
                    {"rep": lax.rem(copy + k, reps)},
                )
            )
        )
    ring_pass(0, 2)
    ring_pass(3, 2)
    for s in range(steps):
        for k in range(1, reps):
            origin = lax.rem(copy + reps - k, reps)
            shared[k, s].wait_recv()
            begin(
                remote(
                    share_all.at[owners[s], origin],
                    share_all.at[owners[s], origin],
                    pass_sent.at[k - 1, s],
                    pass_got.at[k - 1, s],
                    {"fsdp": twin},
                )
            )
    for s in range(3, steps):
        ring_pass(0, s)
        ring_pass(3, s)
    for one in everything:
        one.wait_send()
    for j in range(4):
        for s in range(steps):
            remote(
                inputs[j],
                spot(j, owners[s]),
                twin_sent.at[j, s],
                twin_got.at[j, s],
                {"fsdp": twin},
            ).wait_recv()
    for one in crossed:
        one.wait_recv()
    for k in range(1, reps):
        for s in range(steps):
            remote(
                share,
                share_all.at[owners[s], copy],
                pass_sent.at[k - 1, s],
                pass_got.at[k - 1, s],
                {"fsdp": twin},
            ).wait_recv()
    for one in locals_[:3]:
        one.wait()


def gather_all(token, strip, share, small, reps):
    devices, piece, columns = strip.shape
    steps = devices // 2
    dma = pltpu.SemaphoreType.DMA
    anywhere = pl.BlockSpec(memory_space=pl.ANY)
    return pl.pallas_call(
        functools.partial(gather_kernel, devices, reps),
        in_specs=[pl.BlockSpec(memory_space=pltpu.VMEM)] * 4,
        out_specs=[anywhere] * 4,
        out_shape=[
            jax.ShapeDtypeStruct((devices,) + token.shape, LOW),
            jax.ShapeDtypeStruct((devices, reps, piece, columns), LOW),
            jax.ShapeDtypeStruct((devices, reps) + share.shape, LOW),
            jax.ShapeDtypeStruct((devices,) + small.shape, LOW),
        ],
        scratch_shapes=[
            dma((4, steps)),
            dma((4, steps)),
            dma((4, steps)),
            dma((4, steps)),
            dma((devices - 1,)),
            dma((devices - 1,)),
            dma((reps - 1,)),
            dma((reps - 1,)),
            dma((reps - 1, steps)),
            dma((reps - 1, steps)),
            dma((reps - 1, steps)),
            dma((reps - 1, steps)),
            dma((4,)),
        ],
        cost_estimate=work(100),
        compiler_params=pltpu.CompilerParams(collective_id=0, has_side_effects=True),
    )(token, strip, share, small)


def reduce_rep(values):
    return lax.psum(values, "rep")


def shards(
    tokens,
    lengths,
    dealing,
    routes,
    cotangent,
    first_gain,
    projection,
    projection_bias,
    output_weight,
    second_gain,
    router_weight,
    shared_gate,
    shared_in,
    shared_out,
    expert_in,
    expert_out,
):
    width = tokens.shape[1]
    rows = tokens.shape[0]
    group = dealing.shape[0]
    devices = group // rows
    part = width // devices
    held = part // HEAD_DIM
    experts, _, _, units = expert_in.shape
    hidden = -(-units // 16) * 16
    common = shared_out.shape[0]
    total = common + experts * hidden
    reps = lax.axis_size("rep")
    piece = part // reps
    mine = lax.axis_index("fsdp")
    copy = lax.axis_index("rep")
    scale = HEAD_DIM ** (-0.5)

    gain_one = first_gain.astype(WIDE)
    strip = lax.dynamic_slice_in_dim(projection, copy * piece, piece, 0).astype(WIDE)
    strip = (lax.dynamic_slice_in_dim(gain_one, copy * piece, piece, 0)[:, None] * strip).astype(LOW)
    strip = strip.reshape(piece, 3, devices, part).transpose(2, 0, 1, 3)
    strip = strip.reshape(devices, piece, 3 * part)
    share = lax.dynamic_slice_in_dim(output_weight, copy * piece, piece, 0)
    small = jnp.concatenate(
        [second_gain, shared_gate, projection_bias, router_weight.reshape(-1)]
    )
    length = small.shape[0]
    small = jnp.pad(small, (0, -length % 2048)).reshape(-1, 128)
    token_all, strip, share, small = gather_all(tokens, strip, share, small, reps)
    token_all = token_all.reshape(group, width)
    weight_mine = strip.reshape(width, 3 * part)
    weight_output = share.reshape(width, width)
    small = small.reshape(devices, -1)[:, :length]
    cot_in, _ = lax.optimization_barrier((cotangent, token_all))
    steps = devices // 2
    cot_blocks = ring_blocks(cot_in, devices, 0, 1)

    gain_two = small[:, :part].reshape(width).astype(WIDE)
    gate_weight = small[:, part : 2 * part].reshape(width, 1)
    bias = small[:, 2 * part : 5 * part].reshape(3, devices, part)
    bias_mine = lax.dynamic_slice_in_dim(bias, mine, 1, 1).reshape(3 * part).astype(WIDE)
    router = small[:, 5 * part :].reshape(width, experts)
    choice_weight = jnp.concatenate(
        [gate_weight, router, jnp.zeros((width, 127 - experts), LOW)], axis=1
    )
    scale_all = scale_of(token_all.astype(WIDE))
    projected = scale_all * mm(token_all, weight_mine) + bias_mine
    first_length = lengths[0, 0]
    second = (dealing >= first_length).astype(jnp.int32)
    cosine, sine = rope_tables(dealing - second * first_length)
    shape = (devices, rows, HEAD_DIM)
    cosine = jnp.concatenate([cosine, cosine], axis=1).reshape(shape)
    sine = jnp.concatenate([-sine, sine], axis=1).reshape(shape)
    size = 256 // devices
    at_col = jnp.broadcast_to(dealing.reshape(devices, rows, 1), shape)
    at_row = dealing.reshape(devices, rows // size, size).transpose(1, 0, 2)
    at_row = at_row.reshape(rows // size, 1, devices * size)
    scale_row = jnp.broadcast_to(scale_all.reshape(devices, rows, 1), shape)
    projected, first_step = lax.optimization_barrier((projected, cot_blocks[1]))
    cot_blocks = [cot_blocks[0]] + ring_blocks(first_step, devices, 1, steps // 2)
    query, keyed, value, attended_mine, log_total = attend(
        lengths[0], projected.reshape(devices, rows, 3 * part), cosine, sine, at_col, at_row,
        held, size,
    )
    attended = attended_mine.reshape(group, part)
    cot_blocks = cot_blocks[:-1] + ring_blocks(cot_blocks[-1], devices, steps // 2, steps - 1)
    cot_all = ring_place(cot_blocks, devices).reshape(group, width)
    full = -(-total // 128) * 128
    shared_in, shared_out, expert_in, expert_out, _ = lax.optimization_barrier(
        (shared_in, shared_out, expert_in, expert_out, attended_mine)
    )
    expert_rows = expert_in.transpose(0, 1, 3, 2)
    expert_down = expert_out
    if hidden > units:
        expert_rows = jnp.pad(expert_rows, ((0, 0), (0, 0), (0, hidden - units), (0, 0)))
        expert_down = jnp.pad(expert_down, ((0, 0), (0, hidden - units), (0, 0)))
    fill = jnp.zeros((full - total, width), LOW)
    weights = []
    for half in range(2):
        weights.append(shared_in[half].T)
        weights.append(expert_rows[:, half].reshape(experts * hidden, width))
        weights.append(fill)
    weights = jnp.concatenate(weights + [choice_weight.T], axis=0)
    weight_down = jnp.concatenate(
        [shared_out, expert_down.reshape(experts * hidden, width), fill], axis=0
    )

    attended = lax.all_to_all(attended, "fsdp", split_axis=0, concat_axis=1, tiled=True)

    residual = tokens.astype(WIDE) + mm(attended, weight_output)
    scale_two = scale_of(residual)
    unit = residual * scale_two
    hidden_two = (unit * gain_two).astype(LOW)
    lane = jnp.arange(128, dtype=jnp.int32)
    chosen = jnp.any(routes[:, :, None] + 1 == lane[None, None, :], axis=1).astype(LOW)
    owner = jnp.concatenate(
        [
            jnp.zeros((common,), jnp.int32),
            1 + jnp.repeat(jnp.arange(experts, dtype=jnp.int32), hidden),
            jnp.full((full - total,), 127, jnp.int32),
        ]
    )
    spread = (owner[None, :] == lane[:, None]).astype(LOW)
    hidden_all, act_low, grads = middle(
        hidden_two,
        cot_all.reshape(devices, rows, width),
        weights,
        weight_down,
        chosen.reshape(devices, rows, 128),
        spread,
        experts,
    )
    hidden_all = hidden_all.reshape(group, width)
    act_low = act_low.reshape(group, full)
    grads = grads.reshape(group, 2 * full + 128)

    down_grad = mm_tn(act_low, cot_all, LOW)
    grads, down_grad = lax.optimization_barrier((grads, down_grad))
    down_grad = reduce_rep(down_grad)
    hidden_back = mm(grads, weights, LOW)
    act_low, grads, hidden_back = lax.optimization_barrier((act_low, grads, hidden_back))
    hidden_back = lax.psum_scatter(hidden_back, "fsdp", scatter_dimension=0, tiled=True)
    hidden_back = hidden_back.astype(WIDE)
    in_grad = mm_tn(grads, hidden_all, LOW)
    choice_weight_grad = in_grad[2 * full :].T
    in_grad = jnp.concatenate([in_grad[:total], in_grad[full : full + total]], axis=0)
    in_grad, down_grad = lax.optimization_barrier((in_grad, down_grad))
    in_grad = reduce_rep(in_grad)
    layered = mm(act_low, weight_down, LOW)

    gain_two_grad = jnp.sum(hidden_back * unit, axis=0)
    pushed = hidden_back * gain_two
    residual_grad = cotangent.astype(WIDE) + scale_two * (
        pushed - unit * jnp.mean(pushed * unit, axis=-1, keepdims=True)
    )
    output_low = residual_grad.astype(LOW)
    attended_back = mm_nt(output_low, weight_output, LOW)
    attended_back = lax.all_to_all(
        attended_back, "fsdp", split_axis=1, concat_axis=0, tiled=True
    ).reshape(devices, rows, part)
    attended_back, attended_held = lax.optimization_barrier((attended_back, attended))
    lane = jnp.arange(128, dtype=jnp.int32)
    extra = jnp.where(
        lane[None, :] == experts + 1, gain_two_grad[:, None].astype(LOW), choice_weight_grad
    )
    output_grad = jnp.concatenate([mm_tn(attended_held, output_low, LOW), extra], axis=1)
    output_grad = lax.psum_scatter(output_grad, "fsdp", scatter_dimension=0, tiled=True)

    parts = attend_back(
        lengths[0], query, keyed, value, attended_mine, attended_back, log_total, cosine, sine,
        scale_row, at_col, at_row, held, size,
    )
    projected_back = parts[0].reshape(group, 3 * part)
    scaled_back = parts[1].reshape(group, 3 * part)
    bias_grad = jnp.sum(projected_back.astype(WIDE), axis=0)
    weight_grad = mm_tn(token_all, scaled_back, LOW)
    bias_rows = jnp.broadcast_to(
        bias_grad.astype(LOW).reshape(1, 1, 3, part), (devices, 16, 3, part)
    )
    weight_grad = jnp.concatenate([weight_grad.reshape(devices, part, 3, part), bias_rows], axis=1)
    weight_grad = lax.all_to_all(
        weight_grad, "fsdp", split_axis=0, concat_axis=2, tiled=False
    ).reshape(part + 16, 3 * width)
    weight_grad, projected_back = lax.optimization_barrier((weight_grad, projected_back))
    token_back = mm_nt(projected_back, weight_mine, LOW)
    layered = lax.psum_scatter(layered, "fsdp", scatter_dimension=0, tiled=True)
    output_grad, weight_grad, in_grad, down_grad, layered = lax.optimization_barrier(
        (output_grad, weight_grad, in_grad, down_grad, layered)
    )
    weight_grad, output_grad = reduce_rep((weight_grad, output_grad))
    pushed = lax.psum_scatter(token_back, "fsdp", scatter_dimension=0, tiled=True).astype(WIDE)
    mixed = (residual + layered.astype(WIDE)).astype(LOW)
    bias_grad = weight_grad[part].astype(WIDE).reshape(devices, 3 * part)
    bias_grad = lax.dynamic_slice_in_dim(bias_grad, mine, 1, 0)[0]
    weight_grad = weight_grad[:part].astype(WIDE)
    small = output_grad[:, width:].astype(WIDE)
    output_grad = output_grad[:, :width].astype(WIDE)
    first_gain_grad = jnp.sum(weight_grad * projection.astype(WIDE), axis=1)
    projection_grad = weight_grad * gain_one[:, None]

    inputs = tokens.astype(WIDE)
    scale_one = scale_of(inputs)
    unit_one = inputs * scale_one
    tokens_grad = residual_grad + scale_one * (
        pushed - unit_one * jnp.mean(pushed * unit_one, axis=-1, keepdims=True)
    )

    in_grad = in_grad.reshape(2, total, width)
    shared_in_grad = in_grad[:, :common].astype(WIDE).transpose(0, 2, 1)
    expert_in_grad = in_grad[:, common:].reshape(2, experts, hidden, width)
    expert_in_grad = expert_in_grad[:, :, :units].astype(WIDE).transpose(1, 0, 3, 2)
    down_grad = down_grad.astype(WIDE)
    return (
        mixed,
        tokens_grad,
        first_gain_grad,
        projection_grad,
        bias_grad,
        output_grad,
        small[:, experts + 1],
        small[:, 1 : experts + 1],
        small[:, 0],
        shared_in_grad,
        down_grad[:common],
        expert_in_grad,
        down_grad[common:total].reshape(experts, hidden, width)[:, :units],
    )


def solution(mesh):
    in_specs = (
        P(("rep", "fsdp"), None),
        P("rep", None),
        P("rep"),
        P("rep", None),
        P(("rep", "fsdp"), None),
        P("fsdp"),
        P("fsdp", None),
        P("fsdp"),
        P("fsdp", None),
        P("fsdp"),
        P("fsdp", None),
        P("fsdp"),
        P(None, None, "fsdp"),
        P("fsdp", None),
        P(None, None, None, "fsdp"),
        P(None, "fsdp", None),
    )
    out_specs = (
        P(("rep", "fsdp"), None),
        P(("rep", "fsdp"), None),
        P("fsdp"),
        P("fsdp", None),
        P("fsdp"),
        P("fsdp", None),
        P("fsdp"),
        P("fsdp", None),
        P("fsdp"),
        P(None, None, "fsdp"),
        P("fsdp", None),
        P(None, None, None, "fsdp"),
        P(None, "fsdp", None),
    )
    return jax.shard_map(shards, mesh=mesh, in_specs=in_specs, out_specs=out_specs, check_vma=False)
```
